256 devices in a mesh: row: 16 (over y, z_hi), col: 16 (over z_lo, x, core).
Axes of the slice: x: 4, y: 4, z: 8 (z_hi: 4, z_lo: 2; z = z_hi * 2 + z_lo), core: 2. Of those that a mesh axis runs over, the one named last changes fastest.
Arguments:
- tokens_in: bfloat16 [1024, 12288], P('col', 'row'), may hold values from -6 to 6
- weight_up: bfloat16 [12288, 49152], P('row', 'col'), may hold values from -0.0546875 to 0.0546875
- bias_up: float32 [49152], P('col'), may hold values from -4 to 4
- cotangent: bfloat16 [1024, 49152], P('row', 'col'), may hold values from -0.59765625 to 0.59765625
Outputs:
- activated: bfloat16 [1024, 49152], P('row', 'col')
- grad_tokens: bfloat16 [1024, 12288], P('col', 'row')
- grad_weight: bfloat16 [12288, 49152], P('row', 'col')
- grad_bias: float32 [49152], P('col')
The draws below stay inside these ranges and needn't reach their ends.
All inputs are finite; a program needn't handle non-finite values.
Results may differ from the reference program's by a relative error of at most 0.027.
Values may be sent and summed in bfloat16 or wider, within the bound.
A program may use at most 128 MiB of HBM per device.

```python
import jax
import jax.numpy as jnp
from jax import lax

D = 12288
F = 49152
TOKENS = 1024
N_ROW = 16
N_COL = 16


def shard_levels(rng, shape, pieces, smallest, high):
    level = 1.0
    for dim, parts in pieces:
        steps = jax.random.uniform(jax.random.fold_in(jax.random.fold_in(rng, 6), dim), (parts,), jnp.float32, smallest / len(pieces), high / len(pieces))
        level = level * jnp.repeat(jnp.exp(steps), shape[dim] // parts).reshape((-1,) + (1,) * (len(shape) - 1 - dim))
    return level


def noise(rng, shape, width, reach, pieces=(), held_as=jnp.bfloat16):
    entries = jax.random.normal(rng, shape, jnp.float32) * width
    if len(pieces) > 0:
        entries = shard_levels(rng, shape, pieces, -0.22, 0.18) * entries
    return jnp.clip(entries, min=-reach, max=reach).astype(held_as)


def setup_inputs(seed: int = 0) -> dict:
    arg_keys = jax.random.split(jax.random.key(seed), 5)
    return {
        "tokens_in": noise(arg_keys[0], (TOKENS, D), 1.0, 6.0, ((0, 16), (1, 16))),
        "weight_up": noise(arg_keys[1], (D, F), D ** -0.5, 0.0546875, ((0, 16), (1, 16))),
        "bias_up": noise(arg_keys[2], (F,), 0.5, 4.0, ((0, 16),), jnp.float32),
        "cotangent": noise(arg_keys[3], (TOKENS, F), 0.1, 0.59765625, ((0, 16), (1, 16))),
    }


def gelu_tanh(values):
    return jax.nn.gelu(values, approximate=True)

def reference(tokens_in, weight_up, bias_up, cotangent):
    width_block = D // N_ROW
    hidden_block = F // N_COL

    def forward_step(index, total):
        start = (index * width_block).astype(jnp.int32)
        left = lax.dynamic_slice_in_dim(tokens_in, start, width_block, 1)
        right = lax.dynamic_slice_in_dim(weight_up, start, width_block, 0)
        term = jnp.dot(left, right, preferred_element_type=jnp.float32).astype(jnp.bfloat16)
        term = lax.optimization_barrier(term)
        return total + term.astype(jnp.float32)
    hidden = lax.fori_loop(jnp.int32(0), jnp.int32(N_ROW), forward_step, jnp.zeros((TOKENS, F), jnp.float32)) + bias_up
    outputs, pullback = jax.vjp(gelu_tanh, hidden)
    activated = outputs.astype(jnp.bfloat16)
    grad_hidden = pullback(cotangent.astype(jnp.float32))[0].astype(jnp.bfloat16)

    def backward_step(index, total):
        start = (index * hidden_block).astype(jnp.int32)
        left = lax.dynamic_slice_in_dim(grad_hidden, start, hidden_block, 1)
        right = lax.dynamic_slice_in_dim(weight_up, start, hidden_block, 1)
        term = lax.dot_general(left, right, (((1,), (1,)), ((), ())), preferred_element_type=jnp.float32).astype(jnp.bfloat16)
        term = lax.optimization_barrier(term)
        return total + term.astype(jnp.float32)
    grad_tokens = lax.fori_loop(jnp.int32(0), jnp.int32(N_COL), backward_step, jnp.zeros((TOKENS, D), jnp.float32)).astype(jnp.bfloat16)
    grad_weight = lax.dot_general(tokens_in, grad_hidden, (((0,), (0,)), ((), ())), preferred_element_type=jnp.float32).astype(jnp.bfloat16)
    grad_bias = lax.optimization_barrier(jnp.sum(grad_hidden.astype(jnp.float32), axis=0))
    return (activated, grad_tokens, grad_weight, grad_bias)
```

```python
import functools

import jax
import jax.numpy as jnp
from jax import lax
from jax.experimental import pallas as pl
from jax.experimental.pallas import tpu as pltpu
from jax.sharding import PartitionSpec as P

MESH = pl.DeviceIdType.MESH
BF16 = jnp.bfloat16
F32 = jnp.float32
TOK, DB, FB, BLK = 1024, 768, 3072, 64
KINDS = ("z", "y", "y", "y", "y", "y")
J = len(KINDS)
W = FB // J
GELU_C = 0.7978845608028654
GELU_A = 0.044715


def schedule():
    order = []
    for t in range(J + 5):
        for step, lag in (("F1", 0), ("F2", 0), ("F5", 1), ("F6", 2), ("F3", 0), ("F7", 2), ("F8", 3), ("F9", 4)):
            if 0 <= t - lag < J:
                order.append((step, t - lag))
    return order


def kernel(
    tok_in, w_in, b_in, cot_in, act_out, gt_out, gw_out, gb_out,
    tok, tokt, wv, cot, bias, part, ra, rb, mine, zs, zr, zo, gh, act, gw, gb, gtacc, gts, gpr, gx, gxr, gto,
    lsem, ssem, rsem,
):
    row, col = lax.axis_index("row"), lax.axis_index("col")
    y, zh = row // 4, row % 4
    q, core = col // 2, col % 2
    other = 1 - core

    sends, used = [], {"r": 0, "l": 0}

    def remote(src, dst, device):
        i = used["r"]
        used["r"] += 1
        copy = pltpu.make_async_remote_copy(
            src_ref=src, dst_ref=dst, send_sem=ssem.at[i], recv_sem=rsem.at[i], device_id=device, device_id_type=MESH
        )
        copy.start()
        sends.append(copy)
        return copy

    def local(src, dst):
        i = used["l"]
        used["l"] += 1
        copy = pltpu.make_async_copy(src, dst, lsem.at[i])
        copy.start()
        return copy

    partner = (row, q * 2 + other)

    def chip(d):
        return lax.rem(q + d, 8)

    own_tok = local(tok_in, tok.at[col // 4, col % 4])
    w_loads = [local(w_in.at[:, pl.ds(j * W, W)], wv.at[j]) for j in range(J)]
    cot_load = local(cot_in, cot)
    bias_load = local(b_in, bias)

    barrier = pltpu.get_barrier_semaphore()
    peers = [(lax.rem(row + 4 * d, 16), col) for d in (1, 2, 3)]
    peers += [(y * 4 + lax.rem(zh + d, 4), col) for d in (1, 2, 3)]
    peers += [(row, chip(d) * 2 + core) for d in range(1, 8)] + [partner]
    for peer in peers:
        pl.semaphore_signal(barrier, inc=1, device_id=peer, device_id_type=MESH)
    pl.semaphore_wait(barrier, len(peers))

    direct = [remote(tok_in, tok.at[col // 4, col % 4], (row, chip(d) * 2 + core)) for d in range(1, 8)]
    passed = [remote(tok_in, tok.at[col // 4, col % 4], partner)]
    for d in range(1, 8):
        direct[d - 1].wait_recv()
        k = chip(8 - d) * 2 + core
        passed.append(remote(tok.at[k // 4, k % 4], tok.at[k // 4, k % 4], partner))
    for copy in passed:
        copy.wait_recv()
    own_tok.wait()

    def geometry(j):
        return (y, zh, 4, 1) if KINDS[j] == "y" else (zh, y, 1, 4)

    def near(i, d):
        return lax.rem(i + 4 + d, 4)

    def block(j, p, s):
        _, _, pm, sm = geometry(j)
        return p * pm + s * sm

    def product(j, p):
        left = tok[p] if KINDS[j] == "y" else tok[:, p]
        return jnp.dot(left.reshape(4 * BLK, DB), wv[j], preferred_element_type=F32).reshape(4, BLK, W)

    done = {}

    def f1(j):
        p, s, _, _ = geometry(j)
        w_loads[j].wait()
        p2 = near(p, 2)
        part[j, p2] = product(j, p2).astype(BF16)
        done["a", j] = [
            remote(part.at[j, p2, pl.ds(0, 2)], ra.at[j, 0], (block(j, near(p, 1), s), col)),
            remote(part.at[j, p2, pl.ds(2, 2)], ra.at[j, 1], (block(j, near(p, -1), s), col)),
        ]

    def f2(j):
        p, s, _, _ = geometry(j)
        up, down = near(p, 1), near(p, -1)
        part[j, up] = product(j, up).astype(BF16)
        done["b", j] = [remote(part.at[j, up, pl.ds(2, 2)], rb.at[j, 0, pl.ds(2, 2)], (block(j, up, s), col))]
        part[j, down] = product(j, down).astype(BF16)
        done["b", j] += [remote(part.at[j, down, pl.ds(0, 2)], rb.at[j, 1, pl.ds(0, 2)], (block(j, down, s), col))]

    def f3(j):
        p, s, _, _ = geometry(j)
        up, down = near(p, 1), near(p, -1)
        for i, (to, at) in enumerate(((up, 0), (down, 2))):
            done["a", j][i].wait_recv()
            part[j, to, pl.ds(at, 2)] = (part[j, to, pl.ds(at, 2)].astype(F32) + ra[j, i].astype(F32)).astype(BF16)
            done["b", j] += [remote(part.at[j, to, pl.ds(at, 2)], rb.at[j, i, pl.ds(at, 2)], (block(j, to, s), col))]

    def f5(j):
        p, s, _, _ = geometry(j)
        mine[...] = product(j, p)
        for copy in done["b", j]:
            copy.wait_recv()

        def total(t):
            return mine[t] + rb[j, 0, t].astype(F32) + rb[j, 1, t].astype(F32)

        done["z", j] = []
        for d in (2, 1, 3):
            t = near(s, d)
            zs[j, d - 1] = total(t).astype(BF16)
            done["z", j] += [remote(zs.at[j, d - 1], zr.at[j, d - 1], (block(j, p, t), col))]
        zo[j] = total(s)

    def f6(j):
        p, s, _, _ = geometry(j)
        k = block(j, p, s)
        columns = pl.ds(j * W, W)
        for copy in done["z", j]:
            copy.wait_recv()
        hidden = zo[j] + zr[j, 0].astype(F32) + zr[j, 1].astype(F32) + zr[j, 2].astype(F32) + bias[:, columns]
        square = hidden * hidden
        tanh = jnp.tanh(GELU_C * hidden * (1.0 + GELU_A * square))
        half = 0.5 * (1.0 + tanh)
        act[j] = (hidden * half).astype(BF16)
        slope = half + 0.5 * hidden * (1.0 - tanh * tanh) * (GELU_C * (1.0 + 3.0 * GELU_A * square))
        gh[j, y, zh] = (cot[:, columns].astype(F32) * slope).astype(BF16)
        mineref = gh.at[j, y, zh]
        done["g", j] = [remote(mineref, mineref, (block(j, p, near(s, d)), col)) for d in (1, 2, 3)]
        done["up", j] = [remote(mineref, mineref, (block(j, near(p, 1), s), col))]
        done["down", j] = [remote(mineref, mineref, (block(j, near(p, -1), s), col))]
        done["act", j] = local(act.at[j], act_out.at[:, columns])

    def f7(j):
        p, s, _, _ = geometry(j)
        for d in (1, 2, 3):
            done["g", j][d - 1].wait_recv()
            k = block(j, p, near(s, -d))
            ref = gh.at[j, k // 4, k % 4]
            done["up", j] += [remote(ref, ref, (block(j, near(p, 1), s), col))]
            done["down", j] += [remote(ref, ref, (block(j, near(p, -1), s), col))]

    def f8(j):
        p, s, _, _ = geometry(j)
        done["far", j] = []
        for d in (0, 1):
            done["up", j][d].wait_recv()
            k = block(j, near(p, -1), near(s, -d))
            ref = gh.at[j, k // 4, k % 4]
            done["far", j] += [remote(ref, ref, (block(j, near(p, 1), s), col))]
        for d in (2, 3):
            done["down", j][d].wait_recv()
            k = block(j, near(p, 1), near(s, -d))
            ref = gh.at[j, k // 4, k % 4]
            done["far", j] += [remote(ref, ref, (block(j, near(p, -1), s), col))]

    def f9(j):
        for d in (0, 1):
            done["down", j][d].wait_recv()
        for d in (2, 3):
            done["up", j][d].wait_recv()
        for copy in done["far", j]:
            copy.wait_recv()
        columns = pl.ds(j * W, W)

        @pl.loop(0, 3)
        def _(i):
            rows = pl.ds(pl.multiple_of(i * 256, 256), 256)
            gw[j, rows] = jnp.dot(tokt[rows], gh[j].reshape(TOK, W), preferred_element_type=F32).astype(BF16)

        done["gw", j] = local(gw.at[j], gw_out.at[:, columns])
        gb[:, columns] = jnp.sum(gh[j].reshape(TOK, W).astype(F32), axis=0, keepdims=True)

        @pl.loop(0, 4)
        def _(i):
            term = lax.dot_general(
                gh[j, i].reshape(4 * BLK, W), wv[j], (((1,), (1,)), ((), ())), preferred_element_type=F32
            ).reshape(4, BLK, DB)
            if j == 0:
                gtacc[i] = term
            else:
                gtacc[i] += term

    steps = dict(F1=f1, F2=f2, F3=f3, F5=f5, F6=f6, F7=f7, F8=f8, F9=f9)
    for step, j in schedule():
        if (step, j) == ("F6", 0):
            cot_load.wait()
            bias_load.wait()
        if (step, j) == ("F9", 0):

            @pl.loop(0, 4)
            def _(i):
                tokt[:, pl.ds(pl.multiple_of(i * 256, 256), 256)] = tok[i].reshape(4 * BLK, DB).T

        steps[step](j)

    @pl.loop(0, 8)
    def _(i):
        k = i * 2 + other
        gts[i] = gtacc[k // 4, k % 4].astype(BF16)

    pair = remote(gts, gpr, partner)
    pair.wait_recv()
    over = []
    for d in range(1, 8):
        i = chip(d)
        k = i * 2 + core
        gx[d - 1] = (gtacc[k // 4, k % 4] + gpr[i].astype(F32)).astype(BF16)
        over.append(remote(gx.at[d - 1], gxr.at[d - 1], (row, k)))
    total = gtacc[col // 4, col % 4] + gpr[q].astype(F32)
    for d in range(1, 8):
        over[d - 1].wait_recv()
        total += gxr[d - 1].astype(F32)
    gto[...] = total.astype(BF16)
    last = [local(gto, gt_out), local(gb, gb_out)]

    for copy in last:
        copy.wait()
    for j in range(J):
        done["act", j].wait()
        done["gw", j].wait()
    for copy in sends:
        copy.wait_send()


def on_device(tokens_in, weight_up, bias_up, cotangent):
    anywhere = pl.BlockSpec(memory_space=pl.ANY)
    v = pltpu.VMEM
    act, gt, gw, gb = pl.pallas_call(
        kernel,
        out_shape=[
            jax.ShapeDtypeStruct((BLK, FB), BF16),
            jax.ShapeDtypeStruct((BLK, DB), BF16),
            jax.ShapeDtypeStruct((DB, FB), BF16),
            jax.ShapeDtypeStruct((1, FB), F32),
        ],
        in_specs=[anywhere] * 4,
        out_specs=[anywhere] * 4,
        scratch_shapes=[
            v((4, 4, BLK, DB), BF16),
            v((DB, TOK), BF16),
            v((J, DB, W), BF16),
            v((BLK, FB), BF16),
            v((1, FB), F32),
            v((J, 4, 4, BLK, W), BF16),
            v((J, 2, 2, BLK, W), BF16),
            v((J, 2, 4, BLK, W), BF16),
            v((4, BLK, W), F32),
            v((J, 3, BLK, W), BF16),
            v((J, 3, BLK, W), BF16),
            v((J, BLK, W), F32),
            v((J, 4, 4, BLK, W), BF16),
            v((J, BLK, W), BF16),
            v((J, DB, W), BF16),
            v((1, FB), F32),
            v((4, 4, BLK, DB), F32),
            v((8, BLK, DB), BF16),
            v((8, BLK, DB), BF16),
            v((7, BLK, DB), BF16),
            v((7, BLK, DB), BF16),
            v((BLK, DB), BF16),
            pltpu.SemaphoreType.DMA((3 * J + 8,)),
            pltpu.SemaphoreType.DMA((24 * J + 24,)),
            pltpu.SemaphoreType.DMA((24 * J + 24,)),
        ],
        compiler_params=pltpu.CompilerParams(collective_id=0, has_side_effects=True, vmem_limit_bytes=60 * 2**20),
        name="updown",
    )(tokens_in, weight_up, bias_up.reshape(1, FB), cotangent)
    return act, gt, gw, gb.reshape(FB)


def solution(mesh):
    return jax.shard_map(
        on_device,
        mesh=mesh,
        in_specs=(P("col", "row"), P("row", "col"), P("col"), P("row", "col")),
        out_specs=(P("row", "col"), P("col", "row"), P("row", "col"), P("col")),
        check_vma=False,
    )
```

```python
import jax
import jax.numpy as jnp
from jax import lax
from jax.experimental import pallas as pl
from jax.experimental.pallas import tpu as pltpu
from jax.sharding import PartitionSpec as P

MESH = pl.DeviceIdType.MESH
BF16 = jnp.bfloat16
F32 = jnp.float32
TOK, DB, FB, BLK = 1024, 768, 3072, 64
H, C = 4, 3
KINDS = "yyyyyyyyyyyy"
J = H * C
R, W = BLK // H, FB // C
GELU_C = 0.7978845608028654
GELU_A = 0.044715

ORDER = (
    ("F1", 0), ("F2u", 0), ("F2d", 0), ("F5d", 0), ("F1", 1), ("F2u", 1), ("F2d", 1), ("F5d", 1), ("F3u", 0), ("F3d", 0),
    ("F1", 2), ("F2u", 2), ("F2d", 2), ("F5d", 2), ("F3u", 1), ("F3d", 1), ("F5A", 0), ("F5B", 0), ("A", 1), ("F1", 3),
    ("F2u", 3), ("F2d", 3), ("F5d", 3), ("F3u", 2), ("F3d", 2), ("F5A", 1), ("F5B", 1), ("F1", 4), ("F2u", 4), ("F2d", 4),
    ("F5d", 4), ("F3u", 3), ("F3d", 3), ("F5A", 2), ("F5B", 2), ("A", 2), ("F1", 5), ("F2u", 5), ("F2d", 5), ("F5d", 5),
    ("F3u", 4), ("F3d", 4), ("F5A", 3), ("F5B", 3), ("F1", 6), ("F2u", 6), ("F2d", 6), ("F5d", 6), ("F3u", 5), ("F3d", 5),
    ("F5A", 4), ("F5B", 4), ("F1", 7), ("F2u", 7), ("F2d", 7), ("F5d", 7), ("F3u", 6), ("F3d", 6), ("F5A", 5), ("F5B", 5),
    ("A", 3), ("F6", 0), ("F1", 8), ("F2u", 8), ("F2d", 8), ("F5d", 8), ("F3u", 7), ("F3d", 7), ("F5A", 6), ("F5B", 6), ("F6", 1),
    ("F1", 9), ("F2u", 9), ("F2d", 9), ("F5d", 9), ("F3u", 8), ("F3d", 8), ("F5A", 7), ("F5B", 7), ("F6", 2), ("F1", 10),
    ("F2u", 10), ("F2d", 10), ("F5d", 10), ("F3u", 9), ("F3d", 9), ("F5A", 8), ("F5B", 8), ("F6", 3), ("F1", 11), ("F2u", 11),
    ("F2d", 11), ("F5d", 11), ("F3u", 10), ("F3d", 10), ("F5A", 9), ("F5B", 9), ("TT", 0), ("F6", 4), ("F7", 0, 0), ("F3u", 11),
    ("F3d", 11), ("F5A", 10), ("F5B", 10), ("F7", 0, 1), ("F7", 0, 3), ("F7", 0, 2), ("F6", 5), ("F7", 1, 0), ("F8", 0, 0),
    ("F5A", 11), ("F5B", 11), ("F8", 0, 3), ("F7", 1, 1), ("F7", 1, 3), ("F8", 0, 1), ("F7", 1, 2), ("F8", 0, 2), ("F6", 6),
    ("F7", 2, 0), ("F8", 1, 0), ("F8", 1, 3), ("F7", 2, 1), ("F7", 2, 3), ("F8", 1, 1), ("F7", 2, 2), ("F8", 1, 2), ("F6", 7),
    ("F9t", 0), ("F7", 3, 0), ("F8", 2, 0), ("F8", 2, 3), ("F7", 3, 1), ("F7", 3, 3), ("F8", 2, 1), ("F7", 3, 2), ("F8", 2, 2),
    ("F6", 8), ("F9t", 1), ("F7", 4, 0), ("F8", 3, 0), ("F8", 3, 3), ("F7", 4, 1), ("F7", 4, 3), ("F8", 3, 1), ("F7", 4, 2),
    ("F8", 3, 2), ("F6", 9), ("F9t", 2), ("T1", 0), ("F7", 5, 0), ("F8", 4, 0), ("F8", 4, 3), ("F7", 5, 1), ("F7", 5, 3),
    ("F7", 5, 2), ("F8", 4, 1), ("F8", 4, 2), ("F6", 10), ("F9t", 3), ("F7", 6, 0), ("F8", 5, 0), ("F8", 5, 3), ("F7", 6, 1),
    ("F7", 6, 3), ("F7", 6, 2), ("F8", 5, 1), ("F8", 5, 2), ("F6", 11), ("F9t", 4), ("F7", 7, 0), ("F8", 6, 0), ("F8", 6, 3),
    ("F7", 7, 1), ("F7", 7, 3), ("F7", 7, 2), ("F8", 6, 1), ("F8", 6, 2), ("F9t", 5), ("T2", 0), ("T1", 1), ("F7", 8, 0),
    ("F8", 7, 0), ("F8", 7, 3), ("F7", 8, 1), ("F7", 8, 3), ("F7", 8, 2), ("F8", 7, 1), ("F8", 7, 2), ("F9t", 6), ("F7", 9, 0),
    ("F8", 8, 0), ("F8", 8, 3), ("F7", 9, 1), ("F7", 9, 3), ("F7", 9, 2), ("F8", 8, 1), ("F8", 8, 2), ("F9t", 7), ("F7", 10, 0),
    ("F8", 9, 0), ("F8", 9, 3), ("F7", 10, 1), ("F7", 10, 3), ("F7", 10, 2), ("F8", 9, 1), ("F8", 9, 2), ("F9t", 8), ("T2", 1),
    ("T1", 2), ("F7", 11, 0), ("F8", 10, 0), ("F8", 10, 3), ("F7", 11, 1), ("F7", 11, 3), ("F7", 11, 2), ("F8", 10, 1),
    ("F8", 10, 2), ("F9t", 9), ("F8", 11, 0), ("F9g", 0, 0), ("F8", 11, 3), ("F9g", 0, 1), ("F8", 11, 1), ("F9g", 0, 2),
    ("F8", 11, 2), ("F9t", 10), ("F9g", 1, 0), ("F9g", 1, 1), ("F9g", 1, 2), ("F9t", 11), ("T2", 2), ("T1", 3), ("F9g", 2, 0),
    ("T2", 3), ("F9g", 2, 1), ("F9g", 2, 2), ("T3", 0), ("T3", 1), ("T3", 2), ("T3", 3),
)


def kernel(
    tok_in, w_in, b_in, cot_in, act, gto, gw, gb,
    tok, tokt, wv, cot, bias, part, ra, rb, mine, zs, zr, zo, gh, gtacc, gts, gpr, gx, gxr,
    lsem, ssem, rsem,
):
    row, col = lax.axis_index("row"), lax.axis_index("col")
    y, zh = row // 4, row % 4
    q, core = col // 2, col % 2
    other = 1 - core

    groups, used = {}, {"r": 0, "l": 0}

    def remote(src, dst, device, *group):
        i = used["r"]
        used["r"] += 1
        copy = pltpu.make_async_remote_copy(
            src_ref=src, dst_ref=dst, send_sem=ssem.at[groups.setdefault(group, len(groups))], recv_sem=rsem.at[i],
            device_id=device, device_id_type=MESH,
        )
        copy.start()
        return copy

    def drain(ref, *group):
        pltpu.make_async_remote_copy(
            src_ref=ref, dst_ref=ref, send_sem=ssem.at[groups[group]], recv_sem=rsem.at[0], device_id=partner, device_id_type=MESH
        ).wait_send()

    def local(src, dst):
        i = used["l"]
        used["l"] += 1
        copy = pltpu.make_async_copy(src, dst, lsem.at[i])
        copy.start()
        return copy

    partner = (row, q * 2 + other)

    def chip(d):
        return lax.rem(q + d, 8)

    own_tok = local(tok_in, tok.at[col // 4, col % 4])
    w_loads = [local(w_in.at[:, pl.ds(c * W, W)], wv.at[c]) for c in range(C)]
    cot_load = local(cot_in, cot)
    bias_load = local(b_in, bias)

    barrier = pltpu.get_barrier_semaphore()
    peers = [(lax.rem(row + 4 * d, 16), col) for d in (1, 2, 3)]
    peers += [(y * 4 + lax.rem(zh + d, 4), col) for d in (1, 2, 3)]
    peers += [(row, chip(d) * 2 + core) for d in range(1, 8)] + [partner]
    for peer in peers:
        pl.semaphore_signal(barrier, inc=1, device_id=peer, device_id_type=MESH)
    pl.semaphore_wait(barrier, len(peers))

    done = {}

    def send_tokens(h):
        rows = pl.ds(h * R, R)
        mineref = tok.at[col // 4, col % 4, rows]
        done["t", h] = [remote(tok_in.at[rows], mineref, (row, chip(d) * 2 + core), "t", h) for d in (1, 7, 2, 6, 3, 5, 4)]
        done["p", h] = [remote(tok_in.at[rows], mineref, partner, "p", h)]

    send_tokens(0)

    def pass_tokens(h):
        for i, d in enumerate((1, 7, 2, 6, 3, 5, 4)):
            done["t", h][i].wait_recv()
            k = chip(8 - d) * 2 + core
            ref = tok.at[k // 4, k % 4, pl.ds(h * R, R)]
            done["p", h] += [remote(ref, ref, partner, "p", h)]
        if h + 1 < H:
            send_tokens(h + 1)

    def geometry(j):
        return (y, zh, 4, 1) if KINDS[j] == "y" else (zh, y, 1, 4)

    def near(i, d):
        return lax.rem(i + 4 + d, 4)

    def block(j, p, s):
        _, _, pm, sm = geometry(j)
        return p * pm + s * sm

    def ghref(j, p, s):
        k = block(j, p, s)
        return gh.at[j % C, k // 4, k % 4, pl.ds(j // C * R, R)]

    def product(j, p):
        rows = pl.ds(j // C * R, R)
        left = tok[p, :, rows] if KINDS[j] == "y" else tok[:, p, rows]
        return jnp.dot(left.reshape(4 * R, DB), wv[j % C], preferred_element_type=F32).reshape(4, R, W)

    def keep(j, p):
        _, s, _, _ = geometry(j)
        blocks = product(j, p).astype(BF16)
        for t in range(4):
            part[j, p, near(t - s, 3)] = blocks[t]

    def step_a(h):
        pass_tokens(h)

    def f1(j):
        p, s, _, _ = geometry(j)
        h, c = j // C, j % C
        if h == 0:
            w_loads[c].wait()
        if c == 0:
            for copy in done["p", h]:
                copy.wait_recv()
            if h == 0:
                own_tok.wait()
        far = near(p, 2)
        keep(j, far)
        done["a", j] = [
            remote(part.at[j, far, pl.ds(0, 2)], ra.at[j, 0], (block(j, near(p, 1), s), col), "part", j),
            remote(part.at[j, far, pl.ds(2, 2)], ra.at[j, 1], (block(j, near(p, -1), s), col), "part", j),
        ]

    def f2u(j):
        p, s, _, _ = geometry(j)
        up = near(p, 1)
        keep(j, up)
        done["b", j, 0, 1] = remote(part.at[j, up, pl.ds(2, 2)], rb.at[j, 0, pl.ds(2, 2)], (block(j, up, s), col), "part", j)

    def f2d(j):
        p, s, _, _ = geometry(j)
        down = near(p, -1)
        keep(j, down)
        done["b", j, 1, 0] = remote(part.at[j, down, pl.ds(0, 2)], rb.at[j, 1, pl.ds(0, 2)], (block(j, down, s), col), "part", j)

    def f3u(j):
        p, s, _, _ = geometry(j)
        up, half = near(p, 1), pl.ds(0, 2)
        done["a", j][0].wait_recv()
        part[j, up, half] = (part[j, up, half].astype(F32) + ra[j, 0].astype(F32)).astype(BF16)
        done["b", j, 0, 0] = remote(part.at[j, up, half], rb.at[j, 0, half], (block(j, up, s), col), "part", j)

    def f3d(j):
        p, s, _, _ = geometry(j)
        down, half = near(p, -1), pl.ds(2, 2)
        done["a", j][1].wait_recv()
        part[j, down, half] = (part[j, down, half].astype(F32) + ra[j, 1].astype(F32)).astype(BF16)
        done["b", j, 1, 1] = remote(part.at[j, down, half], rb.at[j, 1, half], (block(j, down, s), col), "part", j)

    def f5d(j):
        p, _, _, _ = geometry(j)
        mine[j] = product(j, p)

    def total(j, i):
        _, s, _, _ = geometry(j)
        return mine[j, near(s, i + 1)] + rb[j, 0, i].astype(F32) + rb[j, 1, i].astype(F32)

    def second(j, d):
        p, s, _, _ = geometry(j)
        zs[j, d - 1] = total(j, d - 1).astype(BF16)
        done["z", j, d] = remote(zs.at[j, d - 1], zr.at[j, d - 1], (block(j, p, near(s, d)), col), "zs", j)

    def f5a(j):
        done["b", j, 0, 0].wait_recv()
        done["b", j, 1, 0].wait_recv()
        second(j, 2)
        second(j, 1)

    def f5b(j):
        done["b", j, 0, 1].wait_recv()
        done["b", j, 1, 1].wait_recv()
        second(j, 3)
        zo[j] = total(j, 3)

    def f6(j):
        p, s, _, _ = geometry(j)
        rows, columns = pl.ds(j // C * R, R), pl.ds(j % C * W, W)
        for d in (1, 2, 3):
            done["z", j, d].wait_recv()
        hidden = zo[j] + zr[j, 0].astype(F32) + zr[j, 1].astype(F32) + zr[j, 2].astype(F32) + bias[:, columns]
        square = hidden * hidden
        tanh = jnp.tanh(GELU_C * hidden * (1.0 + GELU_A * square))
        half = 0.5 * (1.0 + tanh)
        slope = half + 0.5 * hidden * (1.0 - tanh * tanh) * (GELU_C * (1.0 + 3.0 * GELU_A * square))
        ref = ghref(j, p, s)
        ref[...] = (cot[rows, columns].astype(F32) * slope).astype(BF16)
        for d in (2, 1, 3):
            done["g", j, d] = remote(ref, ref, (block(j, p, near(s, d)), col), "gz", j)
        act[rows, columns] = (hidden * half).astype(BF16)

    def f7(j, d):
        p, s, _, _ = geometry(j)
        if d > 0:
            done["g", j, d].wait_recv()
        ref = ghref(j, p, near(s, -d))
        done["u", j, d] = remote(ref, ref, (block(j, near(p, 1), s), col), "gy", j)
        done["d", j, d] = remote(ref, ref, (block(j, near(p, -1), s), col), "gy", j)

    def f8(j, d):
        p, s, _, _ = geometry(j)
        if d < 2:
            done["u", j, d].wait_recv()
            ref = ghref(j, near(p, -1), near(s, -d))
            done["f", j, d] = remote(ref, ref, (block(j, near(p, 1), s), col), "gy", j)
        else:
            done["d", j, d].wait_recv()
            ref = ghref(j, near(p, 1), near(s, -d))
            done["f", j, d] = remote(ref, ref, (block(j, near(p, -1), s), col), "gy", j)

    finished = []

    def drain_gather(j):
        rows = pl.ds(j // C * R, R)
        drain(gh.at[j % C, pl.ds(0, 3), :, rows], "gy", j)
        drain(gh.at[j % C, 0, pl.ds(0, 3), rows], "gz", j)

    def f9t(j):
        h, c = j // C, j % C
        first = all(i // C != h for i in finished)
        drain(part.at[j, pl.ds(0, 3)], "part", j)
        drain(zs.at[j], "zs", j)
        if len(finished) >= 2:
            drain_gather(finished[-2])
        finished.append(j)
        for d in range(4):
            done["d" if d < 2 else "u", j, d].wait_recv()
            done["f", j, d].wait_recv()
        left = gh[c, :, :, pl.ds(h * R, R)].reshape(16 * R, W)

        @pl.loop(0, 3)
        def _(i):
            cols = pl.ds(pl.multiple_of(i * 256, 256), 256)
            term = lax.dot_general(left, wv[c, cols], (((1,), (1,)), ((), ())), preferred_element_type=F32).reshape(4, 4, R, 256)
            if first:
                gtacc[h, :, :, :, cols] = term
            else:
                gtacc[h, :, :, :, cols] += term

    def tt(_):
        @pl.loop(0, 4)
        def _(i):
            tokt[:, pl.ds(pl.multiple_of(i * 256, 256), 256)] = tok[i].reshape(4 * BLK, DB).T

    def f9g(c, i):
        columns, rows = pl.ds(c * W, W), pl.ds(i * 256, 256)
        gw[rows, columns] = jnp.dot(tokt[rows], gh[c].reshape(TOK, W), preferred_element_type=F32).astype(BF16)
        if i == 0:
            gb[:, columns] = jnp.sum(gh[c].reshape(TOK, W).astype(F32), axis=0, keepdims=True)

    def t1(h):
        @pl.loop(0, 8)
        def _(i):
            k = i * 2 + other
            gts[h, i] = gtacc[h, k // 4, k % 4].astype(BF16)

        done["pair", h] = remote(gts.at[h], gpr.at[h], partner, "pair", h)

    def t2(h):
        done["pair", h].wait_recv()
        for d in (4, 1, 7, 2, 6, 3, 5):
            i = chip(d)
            k = i * 2 + core
            gx[h, d - 1] = (gtacc[h, k // 4, k % 4] + gpr[h, i].astype(F32)).astype(BF16)
            done["x", h, d] = remote(gx.at[h, d - 1], gxr.at[h, d - 1], (row, k), "x", h)

    def t3(h):
        sum_ = gtacc[h, col // 4, col % 4] + gpr[h, q].astype(F32)
        for d in (1, 7, 2, 6, 3, 5, 4):
            done["x", h, d].wait_recv()
            sum_ += gxr[h, d - 1].astype(F32)
        gto[pl.ds(h * R, R)] = sum_.astype(BF16)

    steps = dict(
        A=step_a, F1=f1, F2u=f2u, F2d=f2d, F3u=f3u, F3d=f3d, F5d=f5d, F5A=f5a, F5B=f5b, F6=f6, F7=f7, F8=f8, F9t=f9t, F9g=f9g,
        TT=tt, T1=t1, T2=t2, T3=t3,
    )
    pass_tokens(0)
    started = False
    for step, *which in ORDER:
        if step == "F6" and not started:
            cot_load.wait()
            bias_load.wait()
            started = True
        steps[step](*which)

    for j in finished[-2:]:
        drain_gather(j)
    for h in range(H):
        drain(gx.at[h], "t", h)
        drain(gts.at[h], "p", h)
        drain(gts.at[h], "pair", h)
        drain(gx.at[h], "x", h)


def deliver(act, gt, gw, gb, act_out, gt_out, gw_out, gb_out, sem):
    pairs = ((gw, gw_out), (act, act_out), (gt, gt_out), (gb, gb_out))
    copies = [pltpu.make_async_copy(a, b, sem.at[i]) for i, (a, b) in enumerate(pairs)]
    for copy in copies:
        copy.start()
    for copy in copies:
        copy.wait()


def on_device(tokens_in, weight_up, bias_up, cotangent):
    anywhere = pl.BlockSpec(memory_space=pl.ANY)
    here = pl.BlockSpec(memory_space=pltpu.VMEM)
    v = pltpu.VMEM
    shapes = [((BLK, FB), BF16), ((BLK, DB), BF16), ((DB, FB), BF16), ((1, FB), F32)]
    results = pl.pallas_call(
        kernel,
        out_shape=[v(*s) for s in shapes],
        in_specs=[anywhere] * 4,
        out_specs=[here] * 4,
        scratch_shapes=[
            v((4, 4, BLK, DB), BF16),
            v((DB, TOK), BF16),
            v((C, DB, W), BF16),
            v((BLK, FB), BF16),
            v((1, FB), F32),
            v((J, 4, 4, R, W), BF16),
            v((J, 2, 2, R, W), BF16),
            v((J, 2, 4, R, W), BF16),
            v((J, 4, R, W), F32),
            v((J, 3, R, W), BF16),
            v((J, 3, R, W), BF16),
            v((J, R, W), F32),
            v((C, 4, 4, BLK, W), BF16),
            v((H, 4, 4, R, DB), F32),
            v((H, 8, R, DB), BF16),
            v((H, 8, R, DB), BF16),
            v((H, 7, R, DB), BF16),
            v((H, 7, R, DB), BF16),
            pltpu.SemaphoreType.DMA((C + 3,)),
            pltpu.SemaphoreType.DMA((4 * J + 4 * H,)),
            pltpu.SemaphoreType.DMA((24 * J + 23 * H,)),
        ],
        compiler_params=pltpu.CompilerParams(collective_id=0, has_side_effects=True, vmem_limit_bytes=58 * 2**20),
        name="updown",
    )(tokens_in, weight_up, bias_up.reshape(1, FB), cotangent)
    act, gt, gw, gb = pl.pallas_call(
        deliver,
        out_shape=[jax.ShapeDtypeStruct(*s) for s in shapes],
        in_specs=[here] * 4,
        out_specs=[anywhere] * 4,
        scratch_shapes=[pltpu.SemaphoreType.DMA((4,))],
        compiler_params=pltpu.CompilerParams(vmem_limit_bytes=2 * 2**20),
        name="deliver",
    )(*[pltpu.with_memory_space_constraint(r, pltpu.VMEM) for r in results])
    return act, gt, gw, gb.reshape(FB)


def solution(mesh):
    return jax.shard_map(
        on_device,
        mesh=mesh,
        in_specs=(P("col", "row"), P("row", "col"), P("col"), P("row", "col")),
        out_specs=(P("row", "col"), P("col", "row"), P("row", "col"), P("col")),
        check_vma=False,
    )
```

```python
import jax
import jax.numpy as jnp
from jax import lax
from jax.experimental import pallas as pl
from jax.experimental.pallas import tpu as pltpu
from jax.sharding import PartitionSpec as P

MESH = pl.DeviceIdType.MESH
BF16 = jnp.bfloat16
F32 = jnp.float32
TOK, DB, FB, BLK = 1024, 768, 3072, 64
H, C = 4, 3
KINDS = "yzyyzyyyyyyy"
J = H * C
R, W = BLK // H, FB // C
GELU_C = 0.7978845608028654
GELU_A = 0.044715

ORDER = (
    ("F1", 0), ("F2u", 0), ("F2d", 0), ("F5d", 0), ("A0", 1), ("F1", 1), ("F2u", 1), ("F2d", 1), ("F5d", 1), ("F3u", 0),
    ("F3d", 0), ("A", 1), ("F1", 2), ("F2u", 2), ("F2d", 2), ("F5d", 2), ("F1", 3), ("F2u", 3), ("F2d", 3), ("A0", 2), ("F5A", 0),
    ("F5d", 3), ("F3u", 2), ("F3d", 2), ("F1", 4), ("F2u", 4), ("F2d", 4), ("F5d", 4), ("A", 2), ("F3u", 3), ("F3d", 3),
    ("F5C", 0), ("F1", 5), ("F2u", 5), ("F2d", 5), ("F5A", 2), ("F5d", 5), ("A0", 3), ("F1", 6), ("F3u", 1), ("F3d", 1),
    ("F2u", 6), ("F2d", 6), ("F5A", 3), ("F5d", 6), ("F3u", 5), ("F3d", 5), ("F5C", 2), ("A", 3), ("F1", 7), ("F2u", 7),
    ("F2d", 7), ("F5d", 7), ("F3u", 6), ("F3d", 6), ("F6", 0), ("F5C", 3), ("F1", 8), ("F2u", 8), ("F2d", 8), ("F5A", 5),
    ("F5d", 8), ("F3u", 7), ("F3d", 7), ("F1", 9), ("F3u", 4), ("F3d", 4), ("F2u", 9), ("F2d", 9), ("F5A", 6), ("F5d", 9),
    ("F3u", 8), ("F3d", 8), ("F5A", 1), ("F6", 2), ("F5C", 5), ("F1", 10), ("F2u", 10), ("F2d", 10), ("F5A", 7), ("F5d", 10),
    ("F3u", 9), ("F3d", 9), ("F6", 3), ("F5C", 6), ("F6R", 0), ("F1", 11), ("F2u", 11), ("F2d", 11), ("F5A", 8), ("F5d", 11),
    ("F7", 0, 0), ("F3u", 10), ("F3d", 10), ("TT", 0), ("F5C", 7), ("F5A", 9), ("F7", 0, 1), ("F7", 0, 3), ("F7", 0, 2),
    ("F3u", 11), ("F3d", 11), ("F5A", 4), ("F6", 5), ("F5C", 8), ("F6R", 2), ("F5A", 10), ("F7", 2, 0), ("F6", 6), ("F5C", 9),
    ("F6R", 3), ("F8", 0, 1), ("F8", 0, 0), ("F8", 0, 2), ("F8", 0, 3), ("F5A", 11), ("F5C", 1), ("F7", 2, 1), ("F7", 2, 3),
    ("F7", 2, 2), ("F7", 3, 0), ("F6", 7), ("F5C", 10), ("F7", 3, 1), ("F7", 3, 3), ("F7", 3, 2), ("F6", 1), ("F7", 1, 0),
    ("F6", 8), ("F5C", 11), ("F6R", 5), ("F8", 2, 1), ("F8", 2, 0), ("F8", 2, 2), ("F8", 2, 3), ("F7", 5, 0), ("F9t", 0),
    ("F6", 9), ("F6R", 6), ("F8", 3, 1), ("F8", 3, 0), ("F8", 3, 2), ("F8", 3, 3), ("F6R", 1), ("F7", 1, 1), ("F7", 1, 3),
    ("F5C", 4), ("F7", 5, 1), ("F7", 5, 3), ("F7", 5, 2), ("F7", 6, 0), ("F6", 10), ("F6R", 7), ("F7", 6, 1), ("F7", 6, 3),
    ("F7", 6, 2), ("F7", 7, 0), ("F6", 4), ("F7", 4, 0), ("F7", 1, 2), ("F9t", 2), ("F6", 11), ("F6R", 8), ("F8", 5, 1),
    ("F8", 5, 0), ("F8", 5, 2), ("F8", 5, 3), ("F7", 7, 1), ("F7", 7, 3), ("F7", 7, 2), ("F7", 8, 0), ("F9t", 3), ("F6R", 9),
    ("F8", 6, 1), ("F8", 6, 0), ("F8", 1, 0), ("F8", 6, 2), ("F8", 6, 3), ("F8", 1, 3), ("F6R", 4), ("F7", 4, 1), ("F7", 4, 3),
    ("F7", 8, 1), ("F7", 8, 3), ("F7", 8, 2), ("F7", 9, 0), ("F6R", 10), ("F8", 7, 1), ("F8", 7, 0), ("F8", 7, 2), ("F8", 7, 3),
    ("F8", 1, 1), ("F7", 9, 1), ("F8", 1, 2), ("F7", 9, 3), ("F9t", 5), ("F7", 9, 2), ("F7", 10, 0), ("F7", 4, 2), ("F6R", 11),
    ("F8", 8, 1), ("F8", 8, 0), ("F8", 8, 2), ("F8", 8, 3), ("F7", 10, 1), ("F7", 10, 3), ("F9t", 6), ("F7", 10, 2),
    ("F7", 11, 0), ("F8", 9, 1), ("F8", 9, 0), ("F8", 4, 0), ("F8", 9, 2), ("F8", 9, 3), ("F8", 4, 3), ("F7", 11, 1),
    ("F7", 11, 3), ("F9t", 7), ("F7", 11, 2), ("F9t", 1), ("T1", 0), ("F8", 10, 1), ("F8", 10, 0), ("F8", 10, 2), ("F8", 10, 3),
    ("F8", 4, 1), ("F8", 4, 2), ("F9t", 8), ("T1", 2), ("F8", 11, 1), ("F8", 11, 0), ("F8", 11, 2), ("F8", 11, 3), ("F9t", 9),
    ("F9t", 4), ("T1", 1), ("T2", 0), ("F9t", 10), ("T2", 2), ("F9t", 11), ("T1", 3), ("F9g", 0, 0), ("F9g", 0, 1), ("F9g", 0, 2),
    ("T2", 1), ("T2Z", 0), ("F9g", 1, 0), ("T2", 3), ("T2Z", 2), ("F9g", 1, 1), ("F9g", 1, 2), ("F9g", 2, 0), ("T2Z", 1),
    ("F9g", 2, 1), ("F9g", 2, 2), ("T3", 0), ("T3", 1), ("T3", 2), ("T3", 3),
)


def kernel(
    tok_in, w_in, b_in, cot_in, act, gto, gw, gb,
    tok, tokt, wv, cot, bias, part, ra, rb, mine, zs, rr, zr, zo, gh, gtacc, gts, gpr, gx, gxr, gsum,
    lsem, ssem, rsem,
):
    row, col = lax.axis_index("row"), lax.axis_index("col")
    y, zh = row // 4, row % 4
    q, core = col // 2, col % 2
    other = 1 - core

    groups, used = {}, {"r": 0, "l": 0}

    def remote(src, dst, device, *group):
        i = used["r"]
        used["r"] += 1
        copy = pltpu.make_async_remote_copy(
            src_ref=src, dst_ref=dst, send_sem=ssem.at[groups.setdefault(group, len(groups))], recv_sem=rsem.at[i],
            device_id=device, device_id_type=MESH,
        )
        copy.start()
        return copy

    def drain(ref, *group):
        pltpu.make_async_remote_copy(
            src_ref=ref, dst_ref=ref, send_sem=ssem.at[groups[group]], recv_sem=rsem.at[0], device_id=partner, device_id_type=MESH
        ).wait_send()

    def local(src, dst):
        i = used["l"]
        used["l"] += 1
        copy = pltpu.make_async_copy(src, dst, lsem.at[i])
        copy.start()
        return copy

    partner = (row, q * 2 + other)

    def chip(d):
        return lax.rem(q + d, 8)

    own_tok = local(tok_in, tok.at[col // 4, col % 4])
    w_loads = [local(w_in.at[:, pl.ds(c * W, W)], wv.at[c]) for c in range(C)]
    cot_load = local(cot_in, cot)
    bias_load = local(b_in, bias)

    barrier = pltpu.get_barrier_semaphore()
    peers = [(lax.rem(row + 4 * d, 16), col) for d in (1, 2, 3)]
    peers += [(y * 4 + lax.rem(zh + d, 4), col) for d in (1, 2, 3)]
    peers += [(row, chip(d) * 2 + core) for d in range(1, 8)] + [partner]
    for peer in peers:
        pl.semaphore_signal(barrier, inc=1, device_id=peer, device_id_type=MESH)
    pl.semaphore_wait(barrier, len(peers))

    done = {}

    zl, x = q // 4, q % 4
    across = (1 - zl) * 4 + x

    def beside(d):
        return zl * 4 + lax.rem(x + d, 4)

    def send_tokens(h):
        rows = pl.ds(h * R, R)
        mineref = tok.at[col // 4, col % 4, rows]
        if h == 0:
            done["t", h] = [remote(tok_in.at[rows], mineref, (row, chip(d) * 2 + core), "t", h) for d in (1, 7, 2, 6, 3, 5, 4)]
            done["p", h] = [remote(tok_in.at[rows], mineref, partner, "p", h)]
            return
        done["t", h] = [remote(tok_in.at[rows], mineref, (row, c * 2 + core), "t", h) for c in (across, beside(1), beside(3), beside(2))]
        done["p", h] = [remote(tok_in.at[rows], mineref, partner, "p", h)]

    def tokref(c, h):
        k = c * 2 + core
        return tok.at[k // 4, k % 4, pl.ds(h * R, R)]

    def relay_tokens(h):
        done["t", h][0].wait_recv()
        ref = tokref(across, h)
        done["tr", h] = [remote(ref, ref, (row, beside(d) * 2 + core), "t", h) for d in (1, 3, 2)]
        done["p", h] += [remote(ref, ref, partner, "p", h)]

    def pass_tokens(h):
        if h == 0:
            for i, d in enumerate((1, 7, 2, 6, 3, 5, 4)):
                done["t", h][i].wait_recv()
                ref = tokref(chip(8 - d), h)
                done["p", h] += [remote(ref, ref, partner, "p", h)]
        else:
            for i, d in enumerate((1, 3, 2)):
                done["t", h][i + 1].wait_recv()
                ref = tokref(beside(4 - d), h)
                done["p", h] += [remote(ref, ref, partner, "p", h)]
            for i, d in enumerate((1, 3, 2)):
                done["tr", h][i].wait_recv()
                ref = tokref((1 - zl) * 4 + lax.rem(x + 4 - d, 4), h)
                done["p", h] += [remote(ref, ref, partner, "p", h)]
        if h + 1 < H:
            send_tokens(h + 1)

    send_tokens(0)

    def geometry(j):
        return (y, zh, 4, 1) if KINDS[j] == "y" else (zh, y, 1, 4)

    def near(i, d):
        return lax.rem(i + 4 + d, 4)

    def block(j, p, s):
        _, _, pm, sm = geometry(j)
        return p * pm + s * sm

    def ghref(j, p, s):
        k = block(j, p, s)
        return gh.at[j % C, k // 4, k % 4, pl.ds(j // C * R, R)]

    def product(j, p):
        rows = pl.ds(j // C * R, R)
        left = tok[p, :, rows] if KINDS[j] == "y" else tok[:, p, rows]
        return jnp.dot(left.reshape(4 * R, DB), wv[j % C], preferred_element_type=F32).reshape(4, R, W)

    def keep(j, p):
        _, s, _, _ = geometry(j)
        blocks = product(j, p).astype(BF16)
        for t in range(4):
            part[j, p, near(t - s, 3)] = blocks[t]

    def f1(j):
        p, s, _, _ = geometry(j)
        h, c = j // C, j % C
        if h == 0:
            w_loads[c].wait()
        if c == 0:
            for copy in done["p", h]:
                copy.wait_recv()
            if h == 0:
                own_tok.wait()
        far = near(p, 2)
        keep(j, far)
        done["a", j] = [
            remote(part.at[j, far, pl.ds(0, 2)], ra.at[j, 0], (block(j, near(p, 1), s), col), "part", j),
            remote(part.at[j, far, pl.ds(2, 2)], ra.at[j, 1], (block(j, near(p, -1), s), col), "part", j),
        ]

    def f2u(j):
        p, s, _, _ = geometry(j)
        up = near(p, 1)
        keep(j, up)
        done["b", j, 0, 1] = remote(part.at[j, up, pl.ds(2, 2)], rb.at[j, 0, pl.ds(2, 2)], (block(j, up, s), col), "part", j)

    def f2d(j):
        p, s, _, _ = geometry(j)
        down = near(p, -1)
        keep(j, down)
        done["b", j, 1, 0] = remote(part.at[j, down, pl.ds(0, 2)], rb.at[j, 1, pl.ds(0, 2)], (block(j, down, s), col), "part", j)

    def f3u(j):
        p, s, _, _ = geometry(j)
        up, half = near(p, 1), pl.ds(0, 2)
        done["a", j][0].wait_recv()
        part[j, up, half] = (part[j, up, half].astype(F32) + ra[j, 0].astype(F32)).astype(BF16)
        done["b", j, 0, 0] = remote(part.at[j, up, half], rb.at[j, 0, half], (block(j, up, s), col), "part", j)

    def f3d(j):
        p, s, _, _ = geometry(j)
        down, half = near(p, -1), pl.ds(2, 2)
        done["a", j][1].wait_recv()
        part[j, down, half] = (part[j, down, half].astype(F32) + ra[j, 1].astype(F32)).astype(BF16)
        done["b", j, 1, 1] = remote(part.at[j, down, half], rb.at[j, 1, half], (block(j, down, s), col), "part", j)

    def f5d(j):
        p, _, _, _ = geometry(j)
        mine[j] = product(j, p)

    def total(j, i):
        _, s, _, _ = geometry(j)
        return mine[j, near(s, i + 1)] + rb[j, 0, i].astype(F32) + rb[j, 1, i].astype(F32)

    def f5a(j):
        p, s, _, _ = geometry(j)
        done["b", j, 0, 0].wait_recv()
        done["b", j, 1, 0].wait_recv()
        zs[j, 1] = total(j, 1).astype(BF16)
        for i, d in enumerate((1, -1)):
            half = pl.ds(i * (W // 2), W // 2)
            done["r", j, i] = remote(zs.at[j, 1, :, half], rr.at[j, i], (block(j, p, near(s, d)), col), "zs", j)

    def f5c(j):
        p, s, _, _ = geometry(j)
        done["b", j, 0, 1].wait_recv()
        done["b", j, 1, 1].wait_recv()
        for i, d in enumerate((1, -1)):
            at = 2 * i
            done["r", j, i].wait_recv()
            whole, extra = total(j, at), rr[j, i].astype(F32)
            left, right = whole[:, : W // 2], whole[:, W // 2 :]
            left, right = (left + extra, right) if i == 0 else (left, right + extra)
            zs[j, at, :, pl.ds(0, W // 2)] = left.astype(BF16)
            zs[j, at, :, pl.ds(W // 2, W // 2)] = right.astype(BF16)
            done["z", j, i] = remote(zs.at[j, at], zr.at[j, i], (block(j, p, near(s, d)), col), "zs", j)
        zo[j] = total(j, 3)

    def f6(j):
        p, s, _, _ = geometry(j)
        rows, columns = pl.ds(j // C * R, R), pl.ds(j % C * W, W)
        for i in (0, 1):
            done["z", j, i].wait_recv()
        hidden = zo[j] + zr[j, 0].astype(F32) + zr[j, 1].astype(F32) + bias[:, columns]
        square = hidden * hidden
        tanh = jnp.tanh(GELU_C * hidden * (1.0 + GELU_A * square))
        half = 0.5 * (1.0 + tanh)
        slope = half + 0.5 * hidden * (1.0 - tanh * tanh) * (GELU_C * (1.0 + 3.0 * GELU_A * square))
        ref = ghref(j, p, s)
        ref[...] = (cot[rows, columns].astype(F32) * slope).astype(BF16)
        for i, d in enumerate((1, -1)):
            done["g", j, i] = remote(ref, ref, (block(j, p, near(s, d)), col), "gz", j)
        act[rows, columns] = (hidden * half).astype(BF16)

    def f6r(j):
        p, s, _, _ = geometry(j)
        for i, d in enumerate((1, -1)):
            done["g", j, i].wait_recv()
            ref = ghref(j, p, near(s, -d)).at[:, pl.ds(i * (W // 2), W // 2)]
            done["h", j, i] = remote(ref, ref, (block(j, p, near(s, d)), col), "gz", j)

    def f7(j, d):
        p, s, _, _ = geometry(j)
        if d == 2:
            done["h", j, 0].wait_recv()
            done["h", j, 1].wait_recv()
        ref = ghref(j, p, near(s, -d))
        done["u", j, d] = remote(ref, ref, (block(j, near(p, 1), s), col), "gy", j)
        done["d", j, d] = remote(ref, ref, (block(j, near(p, -1), s), col), "gy", j)

    def f8(j, d):
        p, s, _, _ = geometry(j)
        if d < 2:
            done["u", j, d].wait_recv()
            ref = ghref(j, near(p, -1), near(s, -d))
            done["f", j, d] = remote(ref, ref, (block(j, near(p, 1), s), col), "gy", j)
        else:
            done["d", j, d].wait_recv()
            ref = ghref(j, near(p, 1), near(s, -d))
            done["f", j, d] = remote(ref, ref, (block(j, near(p, -1), s), col), "gy", j)

    finished = []

    def drain_gather(j):
        rows = pl.ds(j // C * R, R)
        drain(gh.at[j % C, pl.ds(0, 3), :, rows], "gy", j)
        drain(gh.at[j % C, 0, pl.ds(0, 3), rows], "gz", j)

    def f9t(j):
        h, c = j // C, j % C
        first = all(i // C != h for i in finished)
        drain(part.at[j, pl.ds(0, 3)], "part", j)
        drain(zs.at[j], "zs", j)
        if len(finished) >= 2:
            drain_gather(finished[-2])
        finished.append(j)
        for d in range(4):
            done["d" if d < 2 else "u", j, d].wait_recv()
            done["f", j, d].wait_recv()
        left = gh[c, :, :, pl.ds(h * R, R)].reshape(16 * R, W)

        @pl.loop(0, 3)
        def _(i):
            cols = pl.ds(pl.multiple_of(i * 256, 256), 256)
            term = lax.dot_general(left, wv[c, cols], (((1,), (1,)), ((), ())), preferred_element_type=F32).reshape(4, 4, R, 256)
            if first:
                gtacc[h, :, :, :, cols] = term
            else:
                gtacc[h, :, :, :, cols] += term

    def tt(_):
        @pl.loop(0, 4)
        def _(i):
            tokt[:, pl.ds(pl.multiple_of(i * 256, 256), 256)] = tok[i].reshape(4 * BLK, DB).T

    def f9g(c, i):
        columns, rows = pl.ds(c * W, W), pl.ds(i * 256, 256)
        gw[rows, columns] = jnp.dot(tokt[rows], gh[c].reshape(TOK, W), preferred_element_type=F32).astype(BF16)
        if i == 0:
            gb[:, columns] = jnp.sum(gh[c].reshape(TOK, W).astype(F32), axis=0, keepdims=True)

    def t1(h):
        @pl.loop(0, 8)
        def _(i):
            k = i * 2 + other
            gts[h, i] = gtacc[h, k // 4, k % 4].astype(BF16)

        done["pair", h] = remote(gts.at[h], gpr.at[h], partner, "pair", h)

    def share(h, c):
        k = c * 2 + core
        return gtacc[h, k // 4, k % 4] + gpr[h, c].astype(F32)

    def t2(h):
        done["pair", h].wait_recv()
        if h == H - 1:
            for d in (4, 1, 7, 2, 6, 3, 5):
                c = chip(d)
                gx[h, d - 1] = share(h, c).astype(BF16)
                done["x", h, d] = remote(gx.at[h, d - 1], gxr.at[h, d - 1], (row, c * 2 + core), "x", h)
            return
        for d in (2, 1, 3):
            at = 2 * (d - 1)
            gx[h, at] = share(h, beside(d)).astype(BF16)
            gx[h, at + 1] = share(h, (1 - zl) * 4 + lax.rem(x + d, 4)).astype(BF16)
            two = pl.ds(at, 2)
            done["x", h, d] = remote(gx.at[h, two], gxr.at[h, two], (row, beside(d) * 2 + core), "x", h)

    def t2z(h):
        own, far = share(h, q), share(h, across)
        for d in (1, 3, 2):
            done["x", h, d].wait_recv()
            own += gxr[h, 2 * (d - 1)].astype(F32)
            far += gxr[h, 2 * (d - 1) + 1].astype(F32)
        gsum[h] = own
        gx[h, 6] = far.astype(BF16)
        done["xz", h] = remote(gx.at[h, 6], gxr.at[h, 6], (row, across * 2 + core), "x", h)

    def t3(h):
        if h == H - 1:
            sum_ = share(h, q)
            for d in (1, 7, 2, 6, 3, 5, 4):
                done["x", h, d].wait_recv()
                sum_ += gxr[h, d - 1].astype(F32)
        else:
            done["xz", h].wait_recv()
            sum_ = gsum[h] + gxr[h, 6].astype(F32)
        gto[pl.ds(h * R, R)] = sum_.astype(BF16)

    steps = dict(
        A0=relay_tokens, A=pass_tokens, F1=f1, F2u=f2u, F2d=f2d, F3u=f3u, F3d=f3d, F5d=f5d, F5A=f5a, F5C=f5c, F6=f6, F6R=f6r, F7=f7, F8=f8, F9t=f9t, F9g=f9g,
        TT=tt, T1=t1, T2=t2, T2Z=t2z, T3=t3,
    )
    pass_tokens(0)
    started = False
    for step, *which in ORDER:
        if step == "F6" and not started:
            cot_load.wait()
            bias_load.wait()
            started = True
        steps[step](*which)

    for j in finished[-2:]:
        drain_gather(j)
    for h in range(H):
        drain(gx.at[h], "t", h)
        drain(gts.at[h], "p", h)
        drain(gts.at[h], "pair", h)
        drain(gx.at[h], "x", h)


def deliver(act, gt, gw, gb, act_out, gt_out, gw_out, gb_out, sem):
    pairs = ((gw, gw_out), (act, act_out), (gt, gt_out), (gb, gb_out))
    copies = [pltpu.make_async_copy(a, b, sem.at[i]) for i, (a, b) in enumerate(pairs)]
    for copy in copies:
        copy.start()
    for copy in copies:
        copy.wait()


def on_device(tokens_in, weight_up, bias_up, cotangent):
    anywhere = pl.BlockSpec(memory_space=pl.ANY)
    here = pl.BlockSpec(memory_space=pltpu.VMEM)
    v = pltpu.VMEM
    shapes = [((BLK, FB), BF16), ((BLK, DB), BF16), ((DB, FB), BF16), ((1, FB), F32)]
    results = pl.pallas_call(
        kernel,
        out_shape=[v(*s) for s in shapes],
        in_specs=[anywhere] * 4,
        out_specs=[here] * 4,
        scratch_shapes=[
            v((4, 4, BLK, DB), BF16),
            v((DB, TOK), BF16),
            v((C, DB, W), BF16),
            v((BLK, FB), BF16),
            v((1, FB), F32),
            v((J, 4, 4, R, W), BF16),
            v((J, 2, 2, R, W), BF16),
            v((J, 2, 4, R, W), BF16),
            v((J, 4, R, W), F32),
            v((J, 3, R, W), BF16),
            v((J, 2, R, W // 2), BF16),
            v((J, 2, R, W), BF16),
            v((J, R, W), F32),
            v((C, 4, 4, BLK, W), BF16),
            v((H, 4, 4, R, DB), F32),
            v((H, 8, R, DB), BF16),
            v((H, 8, R, DB), BF16),
            v((H, 7, R, DB), BF16),
            v((H, 7, R, DB), BF16),
            v((H - 1, R, DB), F32),
            pltpu.SemaphoreType.DMA((C + 3,)),
            pltpu.SemaphoreType.DMA((4 * J + 4 * H,)),
            pltpu.SemaphoreType.DMA((26 * J + 23 * H,)),
        ],
        compiler_params=pltpu.CompilerParams(collective_id=0, has_side_effects=True, vmem_limit_bytes=58 * 2**20),
        name="updown",
    )(tokens_in, weight_up, bias_up.reshape(1, FB), cotangent)
    act, gt, gw, gb = pl.pallas_call(
        deliver,
        out_shape=[jax.ShapeDtypeStruct(*s) for s in shapes],
        in_specs=[here] * 4,
        out_specs=[anywhere] * 4,
        scratch_shapes=[pltpu.SemaphoreType.DMA((4,))],
        compiler_params=pltpu.CompilerParams(vmem_limit_bytes=2 * 2**20),
        name="deliver",
    )(*[pltpu.with_memory_space_constraint(r, pltpu.VMEM) for r in results])
    return act, gt, gw, gb.reshape(FB)


def solution(mesh):
    return jax.shard_map(
        on_device,
        mesh=mesh,
        in_specs=(P("col", "row"), P("row", "col"), P("col"), P("row", "col")),
        out_specs=(P("row", "col"), P("col", "row"), P("row", "col"), P("col")),
        check_vma=False,
    )
```

```python
import jax
import jax.numpy as jnp
from jax import lax
from jax.experimental import pallas as pl
from jax.experimental.pallas import tpu as pltpu
from jax.sharding import PartitionSpec as P

MESH = pl.DeviceIdType.MESH
BF16 = jnp.bfloat16
F32 = jnp.float32
TOK, DB, FB, BLK = 1024, 768, 3072, 64
H, C = 4, 3
KINDS = "yzyyzyyyyyyy"
J = H * C
R, W = BLK // H, FB // C
GELU_C = 0.7978845608028654
GELU_A = 0.044715

ORDER = (
    ("F1", 0), ("F2u", 0), ("F2d", 0), ("F5d", 0), ("A0", 1), ("F1", 1), ("F2u", 1), ("F2d", 1), ("F5d", 1), ("F3u", 0),
    ("F3d", 0), ("A", 1), ("F1", 2), ("F2u", 2), ("F2d", 2), ("F5d", 2), ("F1", 3), ("F2u", 3), ("F2d", 3), ("A0", 2), ("F5A", 0),
    ("F5d", 3), ("F3u", 2), ("F3d", 2), ("F1", 4), ("F2u", 4), ("F2d", 4), ("F5d", 4), ("A", 2), ("F3u", 3), ("F3d", 3),
    ("F5C", 0), ("F1", 5), ("F2u", 5), ("F2d", 5), ("F5A", 2), ("F5d", 5), ("A0", 3), ("F1", 6), ("F3u", 1), ("F3d", 1),
    ("F2u", 6), ("F2d", 6), ("F5A", 3), ("F5d", 6), ("F3u", 5), ("F3d", 5), ("F5C", 2), ("A", 3), ("F1", 7), ("F2u", 7),
    ("F2d", 7), ("F5d", 7), ("F3u", 6), ("F3d", 6), ("F6", 0), ("F5C", 3), ("F1", 8), ("F2u", 8), ("F2d", 8), ("F5A", 5),
    ("F5d", 8), ("F3u", 7), ("F3d", 7), ("F1", 9), ("F3u", 4), ("F3d", 4), ("F2u", 9), ("F2d", 9), ("F5A", 6), ("F5d", 9),
    ("F3u", 8), ("F3d", 8), ("F5A", 1), ("F6", 2), ("F5C", 5), ("F1", 10), ("F2u", 10), ("F2d", 10), ("F5A", 7), ("F5d", 10),
    ("F3u", 9), ("F3d", 9), ("F6", 3), ("F5C", 6), ("F6R", 0), ("F1", 11), ("F2u", 11), ("F2d", 11), ("F5A", 8), ("F5d", 11),
    ("F7", 0, 0), ("F3u", 10), ("F3d", 10), ("TT", 0), ("F5C", 7), ("F5A", 9), ("F7", 0, 1), ("F7", 0, 3), ("F7", 0, 2),
    ("F3u", 11), ("F3d", 11), ("F5A", 4), ("F6", 5), ("F5C", 8), ("F6R", 2), ("F5A", 10), ("F7", 2, 0), ("F6", 6), ("F5C", 9),
    ("F6R", 3), ("F8", 0, 1), ("F8", 0, 0), ("F8", 0, 2), ("F8", 0, 3), ("F5A", 11), ("F5C", 1), ("F7", 2, 1), ("F7", 2, 3),
    ("F7", 2, 2), ("F7", 3, 0), ("F6", 7), ("F5C", 10), ("F7", 3, 1), ("F7", 3, 3), ("F7", 3, 2), ("F6", 1), ("F7", 1, 0),
    ("F6", 8), ("F5C", 11), ("F6R", 5), ("F8", 2, 1), ("F8", 2, 0), ("F8", 2, 2), ("F8", 2, 3), ("F7", 5, 0), ("F9t", 0),
    ("F6", 9), ("F6R", 6), ("F8", 3, 1), ("F8", 3, 0), ("F8", 3, 2), ("F8", 3, 3), ("F6R", 1), ("F7", 1, 1), ("F7", 1, 3),
    ("F5C", 4), ("F7", 5, 1), ("F7", 5, 3), ("F7", 5, 2), ("F7", 6, 0), ("F6", 10), ("F6R", 7), ("F7", 6, 1), ("F7", 6, 3),
    ("F7", 6, 2), ("F7", 7, 0), ("F6", 4), ("F7", 4, 0), ("F7", 1, 2), ("F9t", 2), ("F6", 11), ("F6R", 8), ("F8", 5, 1),
    ("F8", 5, 0), ("F8", 5, 2), ("F8", 5, 3), ("F7", 7, 1), ("F7", 7, 3), ("F7", 7, 2), ("F7", 8, 0), ("F9t", 3), ("F6R", 9),
    ("F8", 6, 1), ("F8", 6, 0), ("F8", 1, 0), ("F8", 6, 2), ("F8", 6, 3), ("F8", 1, 3), ("F6R", 4), ("F7", 4, 1), ("F7", 4, 3),
    ("F7", 8, 1), ("F7", 8, 3), ("F7", 8, 2), ("F7", 9, 0), ("F6R", 10), ("F8", 7, 1), ("F8", 7, 0), ("F8", 7, 2), ("F8", 7, 3),
    ("F8", 1, 1), ("F7", 9, 1), ("F8", 1, 2), ("F7", 9, 3), ("F9t", 5), ("F7", 9, 2), ("F7", 10, 0), ("F7", 4, 2), ("F6R", 11),
    ("F8", 8, 1), ("F8", 8, 0), ("F8", 8, 2), ("F8", 8, 3), ("F7", 10, 1), ("F7", 10, 3), ("F9t", 6), ("F7", 10, 2),
    ("F7", 11, 0), ("F8", 9, 1), ("F8", 9, 0), ("F8", 4, 0), ("F8", 9, 2), ("F8", 9, 3), ("F8", 4, 3), ("F7", 11, 1),
    ("F7", 11, 3), ("F9t", 7), ("F7", 11, 2), ("F9t", 1), ("T1", 0), ("F8", 10, 1), ("F8", 10, 0), ("F8", 10, 2), ("F8", 10, 3),
    ("F8", 4, 1), ("F8", 4, 2), ("F9t", 8), ("T1", 2), ("F8", 11, 1), ("F8", 11, 0), ("F8", 11, 2), ("F8", 11, 3), ("F9t", 9),
    ("F9t", 4), ("T1", 1), ("T2", 0), ("F9t", 10), ("T2", 2), ("F9t", 11), ("T1", 3), ("F9g", 0, 0), ("F9g", 0, 1), ("F9g", 0, 2),
    ("T2", 1), ("T2Z", 0), ("F9g", 1, 0), ("T2", 3), ("T2Z", 2), ("F9g", 1, 1), ("F9g", 1, 2), ("T2Z", 1), ("F9g", 2, 0),
    ("F9g", 2, 1), ("F9g", 2, 2), ("T3", 0), ("T3", 2), ("T3", 3), ("T3", 1),
)


def kernel(
    tok_in, w_in, b_in, cot_in, act, gto, gw, gb,
    tok, tokt, wv, cot, bias, part, ra, rb, mine, zs, rr, zr, zo, gh, gtacc, gts, gpr, gx, gxr, gsum,
    lsem, ssem, rsem,
):
    row, col = lax.axis_index("row"), lax.axis_index("col")
    y, zh = row // 4, row % 4
    q, core = col // 2, col % 2
    other = 1 - core

    groups, arrivals, used = {}, {}, {"l": 0}

    def remote(src, dst, device, *group, into=None):
        i = arrivals.setdefault(into or ("one", len(arrivals)), len(arrivals))
        copy = pltpu.make_async_remote_copy(
            src_ref=src, dst_ref=dst, send_sem=ssem.at[groups.setdefault(group, len(groups))], recv_sem=rsem.at[i],
            device_id=device, device_id_type=MESH,
        )
        copy.start()
        return copy

    def drain(ref, *group):
        pltpu.make_async_remote_copy(
            src_ref=ref, dst_ref=ref, send_sem=ssem.at[groups[group]], recv_sem=rsem.at[0], device_id=partner, device_id_type=MESH
        ).wait_send()

    def arrived(ref, *into):
        pltpu.make_async_remote_copy(
            src_ref=ref, dst_ref=ref, send_sem=ssem.at[0], recv_sem=rsem.at[arrivals[into]], device_id=partner, device_id_type=MESH
        ).wait_recv()

    def local(src, dst):
        i = used["l"]
        used["l"] += 1
        copy = pltpu.make_async_copy(src, dst, lsem.at[i])
        copy.start()
        return copy

    partner = (row, q * 2 + other)

    def chip(d):
        return lax.rem(q + d, 8)

    own_tok = local(tok_in, tok.at[col // 4, col % 4])
    w_loads = [local(w_in.at[:, pl.ds(c * W, W)], wv.at[c]) for c in range(C)]
    cot_load = local(cot_in, cot)
    bias_load = local(b_in, bias)

    barrier = pltpu.get_barrier_semaphore()
    peers = [(lax.rem(row + 4 * d, 16), col) for d in (1, 2, 3)]
    peers += [(y * 4 + lax.rem(zh + d, 4), col) for d in (1, 2, 3)]
    peers += [(row, chip(d) * 2 + core) for d in range(1, 8)] + [partner]
    for peer in peers:
        pl.semaphore_signal(barrier, inc=1, device_id=peer, device_id_type=MESH)
    pl.semaphore_wait(barrier, len(peers))

    done = {}

    zl, x = q // 4, q % 4
    across = (1 - zl) * 4 + x

    def beside(d):
        return zl * 4 + lax.rem(x + d, 4)

    def send_tokens(h):
        rows = pl.ds(h * R, R)
        mineref = tok.at[col // 4, col % 4, rows]
        if h == 0:
            done["t", h] = [remote(tok_in.at[rows], mineref, (row, chip(d) * 2 + core), "t", h) for d in (1, 7, 2, 6, 3, 5, 4)]
            done["p", h] = [remote(tok_in.at[rows], mineref, partner, "p", h, into=("p", h))]
            return
        done["t", h] = [remote(tok_in.at[rows], mineref, (row, c * 2 + core), "t", h) for c in (across, beside(1), beside(3), beside(2))]
        done["p", h] = [remote(tok_in.at[rows], mineref, partner, "p", h, into=("p", h))]

    def tokref(c, h):
        k = c * 2 + core
        return tok.at[k // 4, k % 4, pl.ds(h * R, R)]

    def relay_tokens(h):
        done["t", h][0].wait_recv()
        ref = tokref(across, h)
        done["tr", h] = [remote(ref, ref, (row, beside(d) * 2 + core), "t", h, into=("tr", h)) for d in (1, 3, 2)]
        done["p", h] += [remote(ref, ref, partner, "p", h, into=("p", h))]

    def pass_tokens(h):
        if h == 0:
            for i, d in enumerate((1, 7, 2, 6, 3, 5, 4)):
                done["t", h][i].wait_recv()
                ref = tokref(chip(8 - d), h)
                done["p", h] += [remote(ref, ref, partner, "p", h, into=("p", h))]
        else:
            for i, d in enumerate((1, 3, 2)):
                done["t", h][i + 1].wait_recv()
                ref = tokref(beside(4 - d), h)
                done["p", h] += [remote(ref, ref, partner, "p", h, into=("p", h))]
            arrived(gxr.at[h, pl.ds(0, 3)], "tr", h)
            for d in (1, 3, 2):
                ref = tokref((1 - zl) * 4 + lax.rem(x + 4 - d, 4), h)
                done["p", h] += [remote(ref, ref, partner, "p", h, into=("p", h))]
        if h + 1 < H:
            send_tokens(h + 1)

    send_tokens(0)

    def geometry(j):
        return (y, zh, 4, 1) if KINDS[j] == "y" else (zh, y, 1, 4)

    def near(i, d):
        return lax.rem(i + 4 + d, 4)

    def block(j, p, s):
        _, _, pm, sm = geometry(j)
        return p * pm + s * sm

    def ghref(j, p, s):
        k = block(j, p, s)
        return gh.at[j % C, k // 4, k % 4, pl.ds(j // C * R, R)]

    def product(j, p):
        rows = pl.ds(j // C * R, R)
        left = tok[p, :, rows] if KINDS[j] == "y" else tok[:, p, rows]
        return jnp.dot(left.reshape(4 * R, DB), wv[j % C], preferred_element_type=F32).reshape(4, R, W)

    def keep(j, p):
        _, s, _, _ = geometry(j)
        blocks = product(j, p).astype(BF16)
        for t in range(4):
            part[j, p, near(t - s, 3)] = blocks[t]

    def f1(j):
        p, s, _, _ = geometry(j)
        h, c = j // C, j % C
        if h == 0:
            w_loads[c].wait()
        if c == 0:
            arrived(gts.at[h], "p", h)
            if h == 0:
                own_tok.wait()
        far = near(p, 2)
        keep(j, far)
        done["a", j] = [
            remote(part.at[j, far, pl.ds(0, 2)], ra.at[j, 0], (block(j, near(p, 1), s), col), "part", j),
            remote(part.at[j, far, pl.ds(2, 2)], ra.at[j, 1], (block(j, near(p, -1), s), col), "part", j),
        ]

    def f2u(j):
        p, s, _, _ = geometry(j)
        up = near(p, 1)
        keep(j, up)
        done["b", j, 0, 1] = remote(part.at[j, up, pl.ds(2, 2)], rb.at[j, 0, pl.ds(2, 2)], (block(j, up, s), col), "part", j, into=("b", j, 1))

    def f2d(j):
        p, s, _, _ = geometry(j)
        down = near(p, -1)
        keep(j, down)
        done["b", j, 1, 0] = remote(part.at[j, down, pl.ds(0, 2)], rb.at[j, 1, pl.ds(0, 2)], (block(j, down, s), col), "part", j, into=("b", j, 0))

    def f3u(j):
        p, s, _, _ = geometry(j)
        up, half = near(p, 1), pl.ds(0, 2)
        done["a", j][0].wait_recv()
        part[j, up, half] = (part[j, up, half].astype(F32) + ra[j, 0].astype(F32)).astype(BF16)
        done["b", j, 0, 0] = remote(part.at[j, up, half], rb.at[j, 0, half], (block(j, up, s), col), "part", j, into=("b", j, 0))

    def f3d(j):
        p, s, _, _ = geometry(j)
        down, half = near(p, -1), pl.ds(2, 2)
        done["a", j][1].wait_recv()
        part[j, down, half] = (part[j, down, half].astype(F32) + ra[j, 1].astype(F32)).astype(BF16)
        done["b", j, 1, 1] = remote(part.at[j, down, half], rb.at[j, 1, half], (block(j, down, s), col), "part", j, into=("b", j, 1))

    def f5d(j):
        p, _, _, _ = geometry(j)
        mine[j] = product(j, p)

    def total(j, i):
        _, s, _, _ = geometry(j)
        return mine[j, near(s, i + 1)] + rb[j, 0, i].astype(F32) + rb[j, 1, i].astype(F32)

    def f5a(j):
        p, s, _, _ = geometry(j)
        arrived(rb.at[j, :, pl.ds(0, 2)], "b", j, 0)
        zs[j, 1] = total(j, 1).astype(BF16)
        for i, d in enumerate((1, -1)):
            half = pl.ds(i * (W // 2), W // 2)
            done["r", j, i] = remote(zs.at[j, 1, :, half], rr.at[j, i], (block(j, p, near(s, d)), col), "zs", j, into=("r", j))

    def f5c(j):
        p, s, _, _ = geometry(j)
        arrived(rb.at[j, :, pl.ds(2, 2)], "b", j, 1)
        arrived(rr.at[j], "r", j)
        for i, d in enumerate((1, -1)):
            at = 2 * i
            whole, extra = total(j, at), rr[j, i].astype(F32)
            left, right = whole[:, : W // 2], whole[:, W // 2 :]
            left, right = (left + extra, right) if i == 0 else (left, right + extra)
            zs[j, at, :, pl.ds(0, W // 2)] = left.astype(BF16)
            zs[j, at, :, pl.ds(W // 2, W // 2)] = right.astype(BF16)
            done["z", j, i] = remote(zs.at[j, at], zr.at[j, i], (block(j, p, near(s, d)), col), "zs", j, into=("z", j))
        zo[j] = total(j, 3)

    def f6(j):
        p, s, _, _ = geometry(j)
        rows, columns = pl.ds(j // C * R, R), pl.ds(j % C * W, W)
        arrived(zr.at[j], "z", j)
        hidden = zo[j] + zr[j, 0].astype(F32) + zr[j, 1].astype(F32) + bias[:, columns]
        square = hidden * hidden
        tanh = jnp.tanh(GELU_C * hidden * (1.0 + GELU_A * square))
        half = 0.5 * (1.0 + tanh)
        slope = half + 0.5 * hidden * (1.0 - tanh * tanh) * (GELU_C * (1.0 + 3.0 * GELU_A * square))
        ref = ghref(j, p, s)
        ref[...] = (cot[rows, columns].astype(F32) * slope).astype(BF16)
        for i, d in enumerate((1, -1)):
            done["g", j, i] = remote(ref, ref, (block(j, p, near(s, d)), col), "gz", j, into=("g", j))
        act[rows, columns] = (hidden * half).astype(BF16)

    def f6r(j):
        p, s, _, _ = geometry(j)
        arrived(gh.at[j % C, 0, pl.ds(0, 2), pl.ds(j // C * R, R)], "g", j)
        for i, d in enumerate((1, -1)):
            ref = ghref(j, p, near(s, -d)).at[:, pl.ds(i * (W // 2), W // 2)]
            done["h", j, i] = remote(ref, ref, (block(j, p, near(s, d)), col), "gz", j, into=("h", j))

    def f7(j, d):
        p, s, _, _ = geometry(j)
        if d == 2:
            arrived(gh.at[j % C, 0, 0, pl.ds(j // C * R, R)], "h", j)
        ref = ghref(j, p, near(s, -d))
        for key, step in (("u", 1), ("d", -1)):
            into = None if (key == "u") == (d < 2) else ("rest", j)
            done[key, j, d] = remote(ref, ref, (block(j, near(p, step), s), col), "gy", j, into=into)

    def f8(j, d):
        p, s, _, _ = geometry(j)
        if d < 2:
            done["u", j, d].wait_recv()
            ref = ghref(j, near(p, -1), near(s, -d))
            done["f", j, d] = remote(ref, ref, (block(j, near(p, 1), s), col), "gy", j, into=("rest", j))
        else:
            done["d", j, d].wait_recv()
            ref = ghref(j, near(p, 1), near(s, -d))
            done["f", j, d] = remote(ref, ref, (block(j, near(p, -1), s), col), "gy", j, into=("rest", j))

    finished = []

    def drain_gather(j):
        rows = pl.ds(j // C * R, R)
        drain(gh.at[j % C, pl.ds(0, 3), :, rows], "gy", j)
        drain(gh.at[j % C, 0, pl.ds(0, 3), rows], "gz", j)

    def f9t(j):
        h, c = j // C, j % C
        first = all(i // C != h for i in finished)
        drain(part.at[j, pl.ds(0, 3)], "part", j)
        drain(zs.at[j], "zs", j)
        if len(finished) >= 2:
            drain_gather(finished[-2])
        finished.append(j)
        arrived(gh.at[c, pl.ds(0, 2), :, pl.ds(h * R, R)], "rest", j)
        left = gh[c, :, :, pl.ds(h * R, R)].reshape(16 * R, W)

        @pl.loop(0, 3)
        def _(i):
            cols = pl.ds(pl.multiple_of(i * 256, 256), 256)
            term = lax.dot_general(left, wv[c, cols], (((1,), (1,)), ((), ())), preferred_element_type=F32).reshape(4, 4, R, 256)
            if first:
                gtacc[h, :, :, :, cols] = term
            else:
                gtacc[h, :, :, :, cols] += term

    def tt(_):
        @pl.loop(0, 4)
        def _(i):
            tokt[:, pl.ds(pl.multiple_of(i * 256, 256), 256)] = tok[i].reshape(4 * BLK, DB).T

    def f9g(c, i):
        columns, rows = pl.ds(c * W, W), pl.ds(i * 256, 256)
        gw[rows, columns] = jnp.dot(tokt[rows], gh[c].reshape(TOK, W), preferred_element_type=F32).astype(BF16)
        if i == 0:
            gb[:, columns] = jnp.sum(gh[c].reshape(TOK, W).astype(F32), axis=0, keepdims=True)

    def t1(h):
        @pl.loop(0, 8)
        def _(i):
            k = i * 2 + other
            gts[h, i] = gtacc[h, k // 4, k % 4].astype(BF16)

        done["pair", h] = remote(gts.at[h], gpr.at[h], partner, "pair", h)

    def share(h, c):
        k = c * 2 + core
        return gtacc[h, k // 4, k % 4] + gpr[h, c].astype(F32)

    def t2(h):
        done["pair", h].wait_recv()
        if h == H - 1:
            for d in (4, 1, 7, 2, 6, 3, 5):
                c = chip(d)
                gx[h, d - 1] = share(h, c).astype(BF16)
                done["x", h, d] = remote(gx.at[h, d - 1], gxr.at[h, d - 1], (row, c * 2 + core), "x", h, into=("x", h))
            return
        for d in (2, 1, 3):
            at = 2 * (d - 1)
            gx[h, at] = share(h, beside(d)).astype(BF16)
            gx[h, at + 1] = share(h, (1 - zl) * 4 + lax.rem(x + d, 4)).astype(BF16)
            two = pl.ds(at, 2)
            done["x", h, d] = remote(gx.at[h, two], gxr.at[h, two], (row, beside(d) * 2 + core), "x", h, into=("x", h))

    def t2z(h):
        own, far = share(h, q), share(h, across)
        arrived(gxr.at[h, pl.ds(0, 6)], "x", h)
        for d in (1, 3, 2):
            own += gxr[h, 2 * (d - 1)].astype(F32)
            far += gxr[h, 2 * (d - 1) + 1].astype(F32)
        gsum[h] = own
        gx[h, 6] = far.astype(BF16)
        done["xz", h] = remote(gx.at[h, 6], gxr.at[h, 6], (row, across * 2 + core), "x", h)

    def t3(h):
        if h == H - 1:
            sum_ = share(h, q)
            arrived(gxr.at[h], "x", h)
            for d in (1, 7, 2, 6, 3, 5, 4):
                sum_ += gxr[h, d - 1].astype(F32)
        else:
            done["xz", h].wait_recv()
            sum_ = gsum[h] + gxr[h, 6].astype(F32)
        gto[pl.ds(h * R, R)] = sum_.astype(BF16)

    steps = dict(
        A0=relay_tokens, A=pass_tokens, F1=f1, F2u=f2u, F2d=f2d, F3u=f3u, F3d=f3d, F5d=f5d, F5A=f5a, F5C=f5c, F6=f6, F6R=f6r, F7=f7, F8=f8, F9t=f9t, F9g=f9g,
        TT=tt, T1=t1, T2=t2, T2Z=t2z, T3=t3,
    )
    pass_tokens(0)
    started = False
    for step, *which in ORDER:
        if step == "F6" and not started:
            cot_load.wait()
            bias_load.wait()
            started = True
        steps[step](*which)

    for j in finished[-2:]:
        drain_gather(j)
    for h in range(H):
        drain(gx.at[h], "t", h)
        drain(gts.at[h], "p", h)
        drain(gts.at[h], "pair", h)
        drain(gx.at[h], "x", h)


def deliver(act, gt, gw, gb, act_out, gt_out, gw_out, gb_out, sem):
    pairs = ((gw, gw_out), (act, act_out), (gt, gt_out), (gb, gb_out))
    copies = [pltpu.make_async_copy(a, b, sem.at[i]) for i, (a, b) in enumerate(pairs)]
    for copy in copies:
        copy.start()
    for copy in copies:
        copy.wait()


def on_device(tokens_in, weight_up, bias_up, cotangent):
    anywhere = pl.BlockSpec(memory_space=pl.ANY)
    here = pl.BlockSpec(memory_space=pltpu.VMEM)
    v = pltpu.VMEM
    shapes = [((BLK, FB), BF16), ((BLK, DB), BF16), ((DB, FB), BF16), ((1, FB), F32)]
    results = pl.pallas_call(
        kernel,
        out_shape=[v(*s) for s in shapes],
        in_specs=[anywhere] * 4,
        out_specs=[here] * 4,
        scratch_shapes=[
            v((4, 4, BLK, DB), BF16),
            v((DB, TOK), BF16),
            v((C, DB, W), BF16),
            v((BLK, FB), BF16),
            v((1, FB), F32),
            v((J, 4, 4, R, W), BF16),
            v((J, 2, 2, R, W), BF16),
            v((J, 2, 4, R, W), BF16),
            v((J, 4, R, W), F32),
            v((J, 3, R, W), BF16),
            v((J, 2, R, W // 2), BF16),
            v((J, 2, R, W), BF16),
            v((J, R, W), F32),
            v((C, 4, 4, BLK, W), BF16),
            v((H, 4, 4, R, DB), F32),
            v((H, 8, R, DB), BF16),
            v((H, 8, R, DB), BF16),
            v((H, 7, R, DB), BF16),
            v((H, 7, R, DB), BF16),
            v((H - 1, R, DB), F32),
            pltpu.SemaphoreType.DMA((C + 3,)),
            pltpu.SemaphoreType.DMA((4 * J + 4 * H,)),
            pltpu.SemaphoreType.DMA((13 * J + 12 * H,)),
        ],
        compiler_params=pltpu.CompilerParams(collective_id=0, has_side_effects=True, vmem_limit_bytes=58 * 2**20),
        name="updown",
    )(tokens_in, weight_up, bias_up.reshape(1, FB), cotangent)
    act, gt, gw, gb = pl.pallas_call(
        deliver,
        out_shape=[jax.ShapeDtypeStruct(*s) for s in shapes],
        in_specs=[here] * 4,
        out_specs=[anywhere] * 4,
        scratch_shapes=[pltpu.SemaphoreType.DMA((4,))],
        compiler_params=pltpu.CompilerParams(vmem_limit_bytes=2 * 2**20),
        name="deliver",
    )(*[pltpu.with_memory_space_constraint(r, pltpu.VMEM) for r in results])
    return act, gt, gw, gb.reshape(FB)


def solution(mesh):
    return jax.shard_map(
        on_device,
        mesh=mesh,
        in_specs=(P("col", "row"), P("row", "col"), P("col"), P("row", "col")),
        out_specs=(P("row", "col"), P("col", "row"), P("row", "col"), P("col")),
        check_vma=False,
    )
```

```python
import jax
import jax.numpy as jnp
from jax import lax
from jax.experimental import pallas as pl
from jax.experimental.pallas import tpu as pltpu
from jax.sharding import PartitionSpec as P

MESH = pl.DeviceIdType.MESH
BF16 = jnp.bfloat16
F32 = jnp.float32
TOK, DB, FB, BLK = 1024, 768, 3072, 64
H, C = 4, 3
KINDS = "yzyyzyyyyyyy"
J = H * C
R, W = BLK // H, FB // C
GELU_C = 0.7978845608028654
GELU_A = 0.044715

ORDER = (
    ("F1", 0), ("F2u", 0), ("F2d", 0), ("F5d", 0), ("A0", 1), ("F1", 1), ("F2u", 1), ("F2d", 1), ("F5d", 1), ("F3u", 0),
    ("F3d", 0), ("A", 1), ("F1", 2), ("F2u", 2), ("F2d", 2), ("F5d", 2), ("F1", 3), ("F2u", 3), ("F2d", 3), ("A0", 2), ("F5A", 0),
    ("F5d", 3), ("F3u", 2), ("F3d", 2), ("F1", 4), ("F2u", 4), ("F2d", 4), ("F5d", 4), ("A", 2), ("F3u", 3), ("F3d", 3),
    ("F5C", 0), ("F1", 5), ("F2u", 5), ("F2d", 5), ("F5A", 2), ("F5d", 5), ("A0", 3), ("F1", 6), ("F3u", 1), ("F3d", 1),
    ("F2u", 6), ("F2d", 6), ("F5A", 3), ("F5d", 6), ("F3u", 5), ("F3d", 5), ("F5C", 2), ("A", 3), ("F1", 7), ("F2u", 7),
    ("F2d", 7), ("F5d", 7), ("F3u", 6), ("F3d", 6), ("F6", 0), ("F5C", 3), ("F1", 8), ("F2u", 8), ("F2d", 8), ("F5A", 5),
    ("F5d", 8), ("F3u", 7), ("F3d", 7), ("F1", 9), ("F3u", 4), ("F3d", 4), ("F2u", 9), ("F2d", 9), ("F5A", 6), ("F5d", 9),
    ("F3u", 8), ("F3d", 8), ("F5A", 1), ("F6", 2), ("F5C", 5), ("F1", 10), ("F2u", 10), ("F2d", 10), ("F5A", 7), ("F5d", 10),
    ("F3u", 9), ("F3d", 9), ("F6", 3), ("F5C", 6), ("F6R", 0), ("F1", 11), ("F2u", 11), ("F2d", 11), ("F5A", 8), ("F5d", 11),
    ("F7", 0, 0), ("F3u", 10), ("F3d", 10), ("TT", 0), ("F5C", 7), ("F5A", 9), ("F7", 0, 1), ("F7", 0, 3), ("F7", 0, 2),
    ("F3u", 11), ("F3d", 11), ("F5A", 4), ("F6", 5), ("F5C", 8), ("F6R", 2), ("F5A", 10), ("F7", 2, 0), ("F6", 6), ("F5C", 9),
    ("F6R", 3), ("F8", 0, 1), ("F8", 0, 0), ("F8", 0, 2), ("F8", 0, 3), ("F5A", 11), ("F5C", 1), ("F7", 2, 1), ("F7", 2, 3),
    ("F7", 2, 2), ("F7", 3, 0), ("F6", 7), ("F5C", 10), ("F7", 3, 1), ("F7", 3, 3), ("F7", 3, 2), ("F6", 1), ("F7", 1, 0),
    ("F6", 8), ("F5C", 11), ("F6R", 5), ("F8", 2, 1), ("F8", 2, 0), ("F8", 2, 2), ("F8", 2, 3), ("F7", 5, 0), ("F9t", 0),
    ("F6", 9), ("F6R", 6), ("F8", 3, 1), ("F8", 3, 0), ("F8", 3, 2), ("F8", 3, 3), ("F6R", 1), ("F7", 1, 1), ("F7", 1, 3),
    ("F5C", 4), ("F7", 5, 1), ("F7", 5, 3), ("F7", 5, 2), ("F7", 6, 0), ("F6", 10), ("F6R", 7), ("F7", 6, 1), ("F7", 6, 3),
    ("F7", 6, 2), ("F7", 7, 0), ("F6", 4), ("F7", 4, 0), ("F7", 1, 2), ("F9t", 2), ("F6", 11), ("F6R", 8), ("F8", 5, 1),
    ("F8", 5, 0), ("F8", 5, 2), ("F8", 5, 3), ("F7", 7, 1), ("F7", 7, 3), ("F7", 7, 2), ("F7", 8, 0), ("F9t", 3), ("F6R", 9),
    ("F8", 6, 1), ("F8", 6, 0), ("F8", 1, 0), ("F8", 6, 2), ("F8", 6, 3), ("F8", 1, 3), ("F6R", 4), ("F7", 4, 1), ("F7", 4, 3),
    ("F7", 8, 1), ("F7", 8, 3), ("F7", 8, 2), ("F7", 9, 0), ("F6R", 10), ("F8", 7, 1), ("F8", 7, 0), ("F8", 7, 2), ("F8", 7, 3),
    ("F8", 1, 1), ("F7", 9, 1), ("F8", 1, 2), ("F7", 9, 3), ("F9t", 5), ("F7", 9, 2), ("F7", 10, 0), ("F7", 4, 2), ("F6R", 11),
    ("F8", 8, 1), ("F8", 8, 0), ("F8", 8, 2), ("F8", 8, 3), ("F7", 10, 1), ("F7", 10, 3), ("F9t", 6), ("F7", 10, 2),
    ("F7", 11, 0), ("F8", 9, 1), ("F8", 9, 0), ("F8", 4, 0), ("F8", 9, 2), ("F8", 9, 3), ("F8", 4, 3), ("F7", 11, 1),
    ("F7", 11, 3), ("F9t", 7), ("F7", 11, 2), ("F9t", 1), ("T1", 0), ("F8", 10, 1), ("F8", 10, 0), ("F8", 10, 2), ("F8", 10, 3),
    ("F8", 4, 1), ("F8", 4, 2), ("F9t", 8), ("T1", 2), ("F8", 11, 1), ("F8", 11, 0), ("F8", 11, 2), ("F8", 11, 3), ("F9t", 9),
    ("F9t", 4), ("T1", 1), ("F9g", 0, 0), ("F9t", 10), ("F9t", 11), ("T1", 3), ("T2", 0), ("F9g", 0, 1), ("T2", 2), ("F9g", 0, 2),
    ("T2", 1), ("T2Z", 0), ("T2", 3), ("T2Z", 2), ("F9g", 1, 0), ("F9g", 1, 1), ("F9g", 1, 2), ("T2Z", 1), ("F9g", 2, 0),
    ("F9g", 2, 1), ("F9g", 2, 2), ("T3", 0), ("T3", 2), ("T3", 3), ("T3", 1),
)


def kernel(
    tok_in, w_in, b_in, cot_in, act, gto, gw, gb,
    tok, tokt, wv, cot, bias, part, ra, rb, mine, zs, rr, zr, zo, gh, gtacc, gts, gpr, gx, gxr, gsum,
    lsem, ssem, rsem,
):
    row, col = lax.axis_index("row"), lax.axis_index("col")
    y, zh = row // 4, row % 4
    q, core = col // 2, col % 2
    other = 1 - core

    groups, arrivals, used = {}, {}, {"l": 0}

    def remote(src, dst, device, *group, into=None):
        i = arrivals.setdefault(into or ("one", len(arrivals)), len(arrivals))
        copy = pltpu.make_async_remote_copy(
            src_ref=src, dst_ref=dst, send_sem=ssem.at[groups.setdefault(group, len(groups))], recv_sem=rsem.at[i],
            device_id=device, device_id_type=MESH,
        )
        copy.start()
        return copy

    def drain(ref, *group):
        pltpu.make_async_remote_copy(
            src_ref=ref, dst_ref=ref, send_sem=ssem.at[groups[group]], recv_sem=rsem.at[0], device_id=partner, device_id_type=MESH
        ).wait_send()

    def arrived(ref, *into):
        pltpu.make_async_remote_copy(
            src_ref=ref, dst_ref=ref, send_sem=ssem.at[0], recv_sem=rsem.at[arrivals[into]], device_id=partner, device_id_type=MESH
        ).wait_recv()

    def local(src, dst):
        i = used["l"]
        used["l"] += 1
        copy = pltpu.make_async_copy(src, dst, lsem.at[i])
        copy.start()
        return copy

    partner = (row, q * 2 + other)

    def chip(d):
        return lax.rem(q + d, 8)

    own_tok = local(tok_in, tok.at[col // 4, col % 4])
    w_loads = [local(w_in.at[:, pl.ds(c * W, W)], wv.at[c]) for c in range(C)]
    cot_load = local(cot_in, cot)
    bias_load = local(b_in, bias)

    barrier = pltpu.get_barrier_semaphore()
    peers = [(lax.rem(row + 4 * d, 16), col) for d in (1, 2, 3)]
    peers += [(y * 4 + lax.rem(zh + d, 4), col) for d in (1, 2, 3)]
    peers += [(row, chip(d) * 2 + core) for d in range(1, 8)] + [partner]
    for peer in peers:
        pl.semaphore_signal(barrier, inc=1, device_id=peer, device_id_type=MESH)
    pl.semaphore_wait(barrier, len(peers))

    done = {}

    zl, x = q // 4, q % 4
    across = (1 - zl) * 4 + x

    def beside(d):
        return zl * 4 + lax.rem(x + d, 4)

    def send_tokens(h):
        rows = pl.ds(h * R, R)
        mineref = tok.at[col // 4, col % 4, rows]
        if h == 0:
            done["t", h] = [remote(tok_in.at[rows], mineref, (row, chip(d) * 2 + core), "t", h) for d in (1, 7, 2, 6, 3, 5, 4)]
            done["p", h] = [remote(tok_in.at[rows], mineref, partner, "p", h, into=("p", h))]
            return
        done["t", h] = [remote(tok_in.at[rows], mineref, (row, c * 2 + core), "t", h) for c in (across, beside(1), beside(3), beside(2))]
        done["p", h] = [remote(tok_in.at[rows], mineref, partner, "p", h, into=("p", h))]

    def tokref(c, h):
        k = c * 2 + core
        return tok.at[k // 4, k % 4, pl.ds(h * R, R)]

    def relay_tokens(h):
        done["t", h][0].wait_recv()
        ref = tokref(across, h)
        done["tr", h] = [remote(ref, ref, (row, beside(d) * 2 + core), "t", h, into=("tr", h)) for d in (1, 3, 2)]
        done["p", h] += [remote(ref, ref, partner, "p", h, into=("p", h))]

    def pass_tokens(h):
        if h == 0:
            for i, d in enumerate((1, 7, 2, 6, 3, 5, 4)):
                done["t", h][i].wait_recv()
                ref = tokref(chip(8 - d), h)
                done["p", h] += [remote(ref, ref, partner, "p", h, into=("p", h))]
        else:
            for i, d in enumerate((1, 3, 2)):
                done["t", h][i + 1].wait_recv()
                ref = tokref(beside(4 - d), h)
                done["p", h] += [remote(ref, ref, partner, "p", h, into=("p", h))]
            arrived(gxr.at[h, pl.ds(0, 3)], "tr", h)
            for d in (1, 3, 2):
                ref = tokref((1 - zl) * 4 + lax.rem(x + 4 - d, 4), h)
                done["p", h] += [remote(ref, ref, partner, "p", h, into=("p", h))]
        if h + 1 < H:
            send_tokens(h + 1)

    send_tokens(0)

    def geometry(j):
        return (y, zh, 4, 1) if KINDS[j] == "y" else (zh, y, 1, 4)

    def near(i, d):
        return lax.rem(i + 4 + d, 4)

    def block(j, p, s):
        _, _, pm, sm = geometry(j)
        return p * pm + s * sm

    def ghref(j, p, s):
        k = block(j, p, s)
        return gh.at[j % C, k // 4, k % 4, pl.ds(j // C * R, R)]

    def product(j, p):
        rows = pl.ds(j // C * R, R)
        left = tok[p, :, rows] if KINDS[j] == "y" else tok[:, p, rows]
        return jnp.dot(left.reshape(4 * R, DB), wv[j % C], preferred_element_type=F32).reshape(4, R, W)

    def keep(j, p):
        _, s, _, _ = geometry(j)
        blocks = product(j, p).astype(BF16)
        for t in range(4):
            part[j, p, near(t - s, 3)] = blocks[t]

    def f1(j):
        p, s, _, _ = geometry(j)
        h, c = j // C, j % C
        if h == 0:
            w_loads[c].wait()
        if c == 0:
            arrived(gts.at[h], "p", h)
            if h == 0:
                own_tok.wait()
        far = near(p, 2)
        keep(j, far)
        done["a", j] = [
            remote(part.at[j, far, pl.ds(0, 2)], ra.at[j, 0], (block(j, near(p, 1), s), col), "part", j // C),
            remote(part.at[j, far, pl.ds(2, 2)], ra.at[j, 1], (block(j, near(p, -1), s), col), "part", j // C),
        ]

    def f2u(j):
        p, s, _, _ = geometry(j)
        up = near(p, 1)
        keep(j, up)
        done["b", j, 0, 1] = remote(part.at[j, up, pl.ds(2, 2)], rb.at[j, 0, pl.ds(2, 2)], (block(j, up, s), col), "part", j // C, into=("b", j, 1))

    def f2d(j):
        p, s, _, _ = geometry(j)
        down = near(p, -1)
        keep(j, down)
        done["b", j, 1, 0] = remote(part.at[j, down, pl.ds(0, 2)], rb.at[j, 1, pl.ds(0, 2)], (block(j, down, s), col), "part", j // C, into=("b", j, 0))

    def f3u(j):
        p, s, _, _ = geometry(j)
        up, half = near(p, 1), pl.ds(0, 2)
        done["a", j][0].wait_recv()
        part[j, up, half] = (part[j, up, half].astype(F32) + ra[j, 0].astype(F32)).astype(BF16)
        done["b", j, 0, 0] = remote(part.at[j, up, half], rb.at[j, 0, half], (block(j, up, s), col), "part", j // C, into=("b", j, 0))

    def f3d(j):
        p, s, _, _ = geometry(j)
        down, half = near(p, -1), pl.ds(2, 2)
        done["a", j][1].wait_recv()
        part[j, down, half] = (part[j, down, half].astype(F32) + ra[j, 1].astype(F32)).astype(BF16)
        done["b", j, 1, 1] = remote(part.at[j, down, half], rb.at[j, 1, half], (block(j, down, s), col), "part", j // C, into=("b", j, 1))

    def f5d(j):
        p, _, _, _ = geometry(j)
        mine[j] = product(j, p)

    def total(j, i):
        _, s, _, _ = geometry(j)
        return mine[j, near(s, i + 1)] + rb[j, 0, i].astype(F32) + rb[j, 1, i].astype(F32)

    def f5a(j):
        p, s, _, _ = geometry(j)
        arrived(rb.at[j, :, pl.ds(0, 2)], "b", j, 0)
        zs[j, 1] = total(j, 1).astype(BF16)
        for i, d in enumerate((1, -1)):
            half = pl.ds(i * (W // 2), W // 2)
            done["r", j, i] = remote(zs.at[j, 1, :, half], rr.at[j, i], (block(j, p, near(s, d)), col), "zs", j // C, into=("r", j))

    def f5c(j):
        p, s, _, _ = geometry(j)
        arrived(rb.at[j, :, pl.ds(2, 2)], "b", j, 1)
        arrived(rr.at[j], "r", j)
        for i, d in enumerate((1, -1)):
            at = 2 * i
            whole, extra = total(j, at), rr[j, i].astype(F32)
            left, right = whole[:, : W // 2], whole[:, W // 2 :]
            left, right = (left + extra, right) if i == 0 else (left, right + extra)
            zs[j, at, :, pl.ds(0, W // 2)] = left.astype(BF16)
            zs[j, at, :, pl.ds(W // 2, W // 2)] = right.astype(BF16)
            done["z", j, i] = remote(zs.at[j, at], zr.at[j, i], (block(j, p, near(s, d)), col), "zs", j // C, into=("z", j))
        zo[j] = total(j, 3)

    def f6(j):
        p, s, _, _ = geometry(j)
        rows, columns = pl.ds(j // C * R, R), pl.ds(j % C * W, W)
        arrived(zr.at[j], "z", j)
        hidden = zo[j] + zr[j, 0].astype(F32) + zr[j, 1].astype(F32) + bias[:, columns]
        square = hidden * hidden
        tanh = jnp.tanh(GELU_C * hidden * (1.0 + GELU_A * square))
        half = 0.5 * (1.0 + tanh)
        slope = half + 0.5 * hidden * (1.0 - tanh * tanh) * (GELU_C * (1.0 + 3.0 * GELU_A * square))
        ref = ghref(j, p, s)
        ref[...] = (cot[rows, columns].astype(F32) * slope).astype(BF16)
        for i, d in enumerate((1, -1)):
            done["g", j, i] = remote(ref, ref, (block(j, p, near(s, d)), col), "gz", j // C, into=("g", j))
        act[rows, columns] = (hidden * half).astype(BF16)

    def f6r(j):
        p, s, _, _ = geometry(j)
        arrived(gh.at[j % C, 0, pl.ds(0, 2), pl.ds(j // C * R, R)], "g", j)
        for i, d in enumerate((1, -1)):
            ref = ghref(j, p, near(s, -d)).at[:, pl.ds(i * (W // 2), W // 2)]
            done["h", j, i] = remote(ref, ref, (block(j, p, near(s, d)), col), "gz", j // C, into=("h", j))

    def f7(j, d):
        p, s, _, _ = geometry(j)
        if d == 2:
            arrived(gh.at[j % C, 0, 0, pl.ds(j // C * R, R)], "h", j)
        ref = ghref(j, p, near(s, -d))
        for key, step in (("u", 1), ("d", -1)):
            into = None if (key == "u") == (d < 2) else ("rest", j)
            done[key, j, d] = remote(ref, ref, (block(j, near(p, step), s), col), "gy", j // C, into=into)

    def f8(j, d):
        p, s, _, _ = geometry(j)
        if d < 2:
            done["u", j, d].wait_recv()
            ref = ghref(j, near(p, -1), near(s, -d))
            done["f", j, d] = remote(ref, ref, (block(j, near(p, 1), s), col), "gy", j // C, into=("rest", j))
        else:
            done["d", j, d].wait_recv()
            ref = ghref(j, near(p, 1), near(s, -d))
            done["f", j, d] = remote(ref, ref, (block(j, near(p, -1), s), col), "gy", j // C, into=("rest", j))

    finished = []

    def f9t(j):
        h, c = j // C, j % C
        first = all(i // C != h for i in finished)
        finished.append(j)
        if sum(i // C == h for i in finished) == C:
            drain(part.at[pl.ds(h * C, C), pl.ds(0, 3)], "part", h)
            drain(zs.at[pl.ds(h * C, C)], "zs", h)
            drain(gx.at[h], "t", h)
            drain(gts.at[h], "p", h)
        arrived(gh.at[c, pl.ds(0, 2), :, pl.ds(h * R, R)], "rest", j)
        left = gh[c, :, :, pl.ds(h * R, R)].reshape(16 * R, W)

        @pl.loop(0, 3)
        def _(i):
            cols = pl.ds(pl.multiple_of(i * 256, 256), 256)
            term = lax.dot_general(left, wv[c, cols], (((1,), (1,)), ((), ())), preferred_element_type=F32).reshape(4, 4, R, 256)
            if first:
                gtacc[h, :, :, :, cols] = term
            else:
                gtacc[h, :, :, :, cols] += term

    def tt(_):
        @pl.loop(0, 4)
        def _(i):
            tokt[:, pl.ds(pl.multiple_of(i * 256, 256), 256)] = tok[i].reshape(4 * BLK, DB).T

    def f9g(c, i):
        columns, rows = pl.ds(c * W, W), pl.ds(i * 256, 256)
        gw[rows, columns] = jnp.dot(tokt[rows], gh[c].reshape(TOK, W), preferred_element_type=F32).astype(BF16)
        if i == 0:
            gb[:, columns] = jnp.sum(gh[c].reshape(TOK, W).astype(F32), axis=0, keepdims=True)

    def t1(h):
        @pl.loop(0, 8)
        def _(i):
            k = i * 2 + other
            gts[h, i] = gtacc[h, k // 4, k % 4].astype(BF16)

        done["pair", h] = remote(gts.at[h], gpr.at[h], partner, "pair", h)

    def share(h, c):
        k = c * 2 + core
        return gtacc[h, k // 4, k % 4] + gpr[h, c].astype(F32)

    def t2(h):
        done["pair", h].wait_recv()
        if h == H - 1:
            for d in (4, 1, 7, 2, 6, 3, 5):
                c = chip(d)
                gx[h, d - 1] = share(h, c).astype(BF16)
                done["x", h, d] = remote(gx.at[h, d - 1], gxr.at[h, d - 1], (row, c * 2 + core), "x", h, into=("x", h))
            return
        for d in (2, 1, 3):
            at = 2 * (d - 1)
            gx[h, at] = share(h, beside(d)).astype(BF16)
            gx[h, at + 1] = share(h, (1 - zl) * 4 + lax.rem(x + d, 4)).astype(BF16)
            two = pl.ds(at, 2)
            done["x", h, d] = remote(gx.at[h, two], gxr.at[h, two], (row, beside(d) * 2 + core), "x", h, into=("x", h))

    def t2z(h):
        own, far = share(h, q), share(h, across)
        arrived(gxr.at[h, pl.ds(0, 6)], "x", h)
        for d in (1, 3, 2):
            own += gxr[h, 2 * (d - 1)].astype(F32)
            far += gxr[h, 2 * (d - 1) + 1].astype(F32)
        gsum[h] = own
        gx[h, 6] = far.astype(BF16)
        done["xz", h] = remote(gx.at[h, 6], gxr.at[h, 6], (row, across * 2 + core), "x", h)

    def t3(h):
        if h == H - 1:
            sum_ = share(h, q)
            arrived(gxr.at[h], "x", h)
            for d in (1, 7, 2, 6, 3, 5, 4):
                sum_ += gxr[h, d - 1].astype(F32)
        else:
            done["xz", h].wait_recv()
            sum_ = gsum[h] + gxr[h, 6].astype(F32)
        gto[pl.ds(h * R, R)] = sum_.astype(BF16)

    steps = dict(
        A0=relay_tokens, A=pass_tokens, F1=f1, F2u=f2u, F2d=f2d, F3u=f3u, F3d=f3d, F5d=f5d, F5A=f5a, F5C=f5c, F6=f6, F6R=f6r, F7=f7, F8=f8, F9t=f9t, F9g=f9g,
        TT=tt, T1=t1, T2=t2, T2Z=t2z, T3=t3,
    )
    pass_tokens(0)
    started = False
    for step, *which in ORDER:
        if step == "F6" and not started:
            cot_load.wait()
            bias_load.wait()
            started = True
        steps[step](*which)

    for h in range(H):
        rows = pl.ds(h * R, R)
        drain(gh.at[:, pl.ds(0, 3), :, rows], "gy", h)
        drain(gh.at[:, 0, pl.ds(0, 3), rows], "gz", h)
        drain(gts.at[h], "pair", h)
        drain(gx.at[h], "x", h)


def deliver(act, gt, gw, gb, act_out, gt_out, gw_out, gb_out, sem):
    pairs = ((gw, gw_out), (act, act_out), (gt, gt_out), (gb, gb_out))
    copies = [pltpu.make_async_copy(a, b, sem.at[i]) for i, (a, b) in enumerate(pairs)]
    for copy in copies:
        copy.start()
    for copy in copies:
        copy.wait()


def on_device(tokens_in, weight_up, bias_up, cotangent):
    anywhere = pl.BlockSpec(memory_space=pl.ANY)
    here = pl.BlockSpec(memory_space=pltpu.VMEM)
    v = pltpu.VMEM
    shapes = [((BLK, FB), BF16), ((BLK, DB), BF16), ((DB, FB), BF16), ((1, FB), F32)]
    results = pl.pallas_call(
        kernel,
        out_shape=[v(*s) for s in shapes],
        in_specs=[anywhere] * 4,
        out_specs=[here] * 4,
        scratch_shapes=[
            v((4, 4, BLK, DB), BF16),
            v((DB, TOK), BF16),
            v((C, DB, W), BF16),
            v((BLK, FB), BF16),
            v((1, FB), F32),
            v((J, 4, 4, R, W), BF16),
            v((J, 2, 2, R, W), BF16),
            v((J, 2, 4, R, W), BF16),
            v((J, 4, R, W), F32),
            v((J, 3, R, W), BF16),
            v((J, 2, R, W // 2), BF16),
            v((J, 2, R, W), BF16),
            v((J, R, W), F32),
            v((C, 4, 4, BLK, W), BF16),
            v((H, 4, 4, R, DB), F32),
            v((H, 8, R, DB), BF16),
            v((H, 8, R, DB), BF16),
            v((H, 7, R, DB), BF16),
            v((H, 7, R, DB), BF16),
            v((H - 1, R, DB), F32),
            pltpu.SemaphoreType.DMA((C + 3,)),
            pltpu.SemaphoreType.DMA((8 * H,)),
            pltpu.SemaphoreType.DMA((13 * J + 12 * H,)),
        ],
        compiler_params=pltpu.CompilerParams(collective_id=0, has_side_effects=True, vmem_limit_bytes=58 * 2**20),
        name="updown",
    )(tokens_in, weight_up, bias_up.reshape(1, FB), cotangent)
    act, gt, gw, gb = pl.pallas_call(
        deliver,
        out_shape=[jax.ShapeDtypeStruct(*s) for s in shapes],
        in_specs=[here] * 4,
        out_specs=[anywhere] * 4,
        scratch_shapes=[pltpu.SemaphoreType.DMA((4,))],
        compiler_params=pltpu.CompilerParams(vmem_limit_bytes=2 * 2**20),
        name="deliver",
    )(*[pltpu.with_memory_space_constraint(r, pltpu.VMEM) for r in results])
    return act, gt, gw, gb.reshape(FB)


def solution(mesh):
    return jax.shard_map(
        on_device,
        mesh=mesh,
        in_specs=(P("col", "row"), P("row", "col"), P("col"), P("row", "col")),
        out_specs=(P("row", "col"), P("col", "row"), P("row", "col"), P("col")),
        check_vma=False,
    )
```
